256 devices in a mesh: dp: 16 (over x, y), seq: 16 (over z, core).
Axes of the slice: x: 4, y: 4, z: 8, core: 2. Of those that a mesh axis runs over, the one named last changes fastest.
Arguments:
- queries: bfloat16 [16, 2048, 2048], P('dp', 'seq'), may hold values from -6 to 6
- attended_grad: bfloat16 [16, 2048, 2048], P('dp', 'seq'), may hold values from -6 to 6
- neighbour_pool: bfloat16 [16, 64, 128, 896], P('dp', 'seq'), may hold values from -6 to 6
- stretch_slot: int32 [16, 32], P('dp'), may hold values from 0 to 63, as said below
- enc_gain: float32 [896], replicated, may hold values from 0.1 to 1.9
- enc_up: bfloat16 [896, 1792], replicated, may hold values from -0.1875 to 0.1875
- enc_down: bfloat16 [1792, 896], replicated, may hold values from -0.125 to 0.125
- key_weight: bfloat16 [896, 2048], P(None, 'seq'), may hold values from -0.1875 to 0.1875
- value_weight: bfloat16 [896, 2048], P(None, 'seq'), may hold values from -0.1875 to 0.1875
Outputs:
- attended: bfloat16 [16, 2048, 2048], P('dp', 'seq')
- query_grad: bfloat16 [16, 2048, 2048], P('dp', 'seq')
- pool_grad: bfloat16 [16, 64, 128, 896], P('dp', 'seq')
- key_weight_grad: float32 [896, 2048], P(None, 'seq')
- value_weight_grad: float32 [896, 2048], P(None, 'seq')
The draws below stay inside these ranges and needn't reach their ends.
Inputs may be any that keep to these rules, and one draw needn't show every extreme that they name: `stretch_slot`: slot s is held by the device s // 4 along seq. No slot is named twice within a sequence, and in every sequence some device holds 4 named slots.
All inputs are finite; a program needn't handle non-finite values.
Results may differ from the reference program's by a relative error of at most 0.03.
Values may be sent and summed in bfloat16 or wider, within the bound.
A program may use at most 128 MiB of HBM per device.

```python
import math
import jax
import jax.numpy as jnp
from jax import lax

STRETCHES_DEV = 2
STRETCH = 64
NLEN = 128
DE = 896
FFE = 1792
HEADS = 16
HD = 128
HQ = 2048
CAP = 4
SLOTS = 64
STRETCHES = 32
L = 2048
SEQS = 16
N_SEQ = 16


def draw_stretch_slot(key, part):
    key = jax.random.fold_in(key, 11)

    def one_sequence(seq_key):
        busy_key, order_key, shuffle_key = jax.random.split(seq_key, 3)
        busiest = jax.random.randint(busy_key, (), 0, SLOTS // CAP)
        order = jax.random.permutation(order_key, SLOTS).astype(jnp.int32)
        slot_rank = jnp.zeros((SLOTS,), jnp.int32).at[order].set(jnp.arange(SLOTS, dtype=jnp.int32))
        elsewhere = (jnp.arange(SLOTS, dtype=jnp.int32) // CAP != busiest).astype(jnp.int32)
        priority = elsewhere * SLOTS + slot_rank
        chosen = jnp.argsort(priority, stable=True)[:STRETCHES].astype(jnp.int32)
        return jax.random.permutation(shuffle_key, chosen).astype(jnp.int32)
    return jax.vmap(one_sequence)(jax.random.split(key, SEQS))


def shard_levels(own_key, dims, cuts, low, high):
    loudness, own = 1.0, jax.random.fold_in(own_key, 6)
    for dim, shards_of in cuts:
        steps = jnp.exp(jax.random.uniform(jax.random.fold_in(own, dim), (shards_of,), jnp.float32, low / len(cuts), high / len(cuts)))
        loudness = loudness * jnp.repeat(steps, dims[dim] // shards_of).reshape([-1 if axis == dim else 1 for axis in range(len(dims))])
    return loudness


def normal_values(own_key, dims, spread, bound, pieces=(), kind=jnp.bfloat16):
    values = jax.random.normal(own_key, dims, jnp.float32) * spread
    if len(pieces) > 0:
        values = shard_levels(own_key, dims, pieces, -0.22, 0.18) * values
    return jnp.clip(values, min=-bound, max=bound).astype(kind)


def setup_inputs(seed: int = 0) -> dict:
    seeds = jax.random.split(jax.random.key(seed), 10)
    return {
        "queries": normal_values(seeds[0], (SEQS, L, HQ), 1.0, 6.0, ((0, 16), (1, 16))),
        "attended_grad": normal_values(seeds[1], (SEQS, L, HQ), 1.0, 6.0, ((0, 16), (1, 16))),
        "neighbour_pool": normal_values(seeds[2], (SEQS, SLOTS, NLEN, DE), 1.0, 6.0, ((0, 16), (1, 16))),
        "stretch_slot": draw_stretch_slot(jax.random.fold_in(seeds[9], 71), 0),
        "enc_gain": jnp.clip(1.0 + 0.18 * jax.random.normal(seeds[4], (DE,), jnp.float32), 0.1, 1.9),
        "enc_up": normal_values(seeds[5], (DE, FFE), DE ** -0.5, 0.1875),
        "enc_down": normal_values(seeds[6], (FFE, DE), FFE ** -0.5, 0.125),
        "key_weight": normal_values(seeds[7], (DE, HQ), DE ** -0.5, 0.1875, ((1, 16),)),
        "value_weight": normal_values(seeds[8], (DE, HQ), DE ** -0.5, 0.1875, ((1, 16),)),
    }


epsilon = 1e-06

def encode_rows(row_block, gain_vector, up_matrix, down_matrix):
    row_values = row_block.astype(jnp.float32)
    inverse = lax.rsqrt(lax.optimization_barrier(jnp.mean(row_values * row_values, axis=-1, keepdims=True)) + epsilon)
    normed = (row_values * inverse * gain_vector).astype(jnp.bfloat16)
    before = jnp.dot(normed, up_matrix, preferred_element_type=jnp.float32)
    activity = jax.nn.gelu(before).astype(jnp.bfloat16)
    encoded = (row_values + jnp.dot(activity, down_matrix, preferred_element_type=jnp.float32)).astype(jnp.bfloat16)
    return (encoded, before, inverse)

def encode_backward(encoded_grad, row_block, before, inverse, gain_vector, up_matrix, down_matrix):
    activity_grad = jnp.dot(encoded_grad, down_matrix.T, preferred_element_type=jnp.float32)
    unused_value, gelu_back = jax.vjp(jax.nn.gelu, before)
    before_grad = gelu_back(activity_grad)[0].astype(jnp.bfloat16)
    normed_grad = jnp.dot(before_grad, up_matrix.T, preferred_element_type=jnp.float32)
    row_values = row_block.astype(jnp.float32)
    scaled_grad = gain_vector * normed_grad
    cubed = inverse * inverse * inverse
    result = encoded_grad.astype(jnp.float32) + inverse * scaled_grad - row_values * cubed * lax.optimization_barrier(jnp.mean(row_values * scaled_grad, axis=-1, keepdims=True))
    return result.astype(jnp.bfloat16)

def sequence_terms(query_seq, grad_seq, pool_seq, slot_seq, enc_gain, enc_up, enc_down, key_weight, value_weight):
    score_scale = 1.0 / math.sqrt(HD)
    used_rows = pool_seq[slot_seq.astype(jnp.int32)].reshape(STRETCHES * NLEN, DE)
    encoded_rows, before, inverse = encode_rows(used_rows, enc_gain, enc_up, enc_down)
    key_rows = jnp.dot(encoded_rows, key_weight, preferred_element_type=jnp.float32).astype(jnp.bfloat16)
    value_rows = jnp.dot(encoded_rows, value_weight, preferred_element_type=jnp.float32).astype(jnp.bfloat16)
    query_blocks = query_seq.reshape(STRETCHES, STRETCH, HEADS, HD).astype(jnp.float32)
    key_blocks = key_rows.reshape(STRETCHES, NLEN, HEADS, HD).astype(jnp.float32)
    value_blocks = value_rows.reshape(STRETCHES, NLEN, HEADS, HD).astype(jnp.float32)
    grad_blocks = grad_seq.reshape(STRETCHES, STRETCH, HEADS, HD).astype(jnp.float32)
    scores = jnp.einsum('cqhe,ckhe->chqk', query_blocks, key_blocks) * score_scale
    exponent = jnp.exp(scores)
    weights = exponent / lax.optimization_barrier(jnp.sum(exponent, axis=-1, keepdims=True))
    probabilities = weights.astype(jnp.bfloat16)
    attended = jnp.einsum('chqk,ckhe->cqhe', probabilities.astype(jnp.float32), value_blocks).astype(jnp.bfloat16).reshape(L, HQ)
    prob_grad = jnp.einsum('cqhe,ckhe->chqk', grad_blocks, value_blocks)
    score_grad = (weights * (prob_grad - lax.optimization_barrier(jnp.sum(weights * prob_grad, axis=-1, keepdims=True))) * score_scale).astype(jnp.bfloat16)
    query_grad = jnp.einsum('chqk,ckhe->cqhe', score_grad.astype(jnp.float32), key_blocks).astype(jnp.bfloat16).reshape(L, HQ)
    key_grad = jnp.einsum('chqk,cqhe->ckhe', score_grad.astype(jnp.float32), query_blocks).astype(jnp.bfloat16).reshape(STRETCHES * NLEN, HQ)
    value_grad = jnp.einsum('chqk,cqhe->ckhe', probabilities.astype(jnp.float32), grad_blocks).astype(jnp.bfloat16).reshape(STRETCHES * NLEN, HQ)
    group_rows = encoded_rows.reshape(N_SEQ, STRETCHES_DEV * NLEN, DE).astype(jnp.float32)
    key_part = jnp.einsum('nrd,nrh->ndh', group_rows, key_grad.reshape(N_SEQ, STRETCHES_DEV * NLEN, HQ).astype(jnp.float32))
    value_part = jnp.einsum('nrd,nrh->ndh', group_rows, value_grad.reshape(N_SEQ, STRETCHES_DEV * NLEN, HQ).astype(jnp.float32))
    key_total = lax.optimization_barrier(jnp.sum(lax.optimization_barrier(key_part.astype(jnp.bfloat16)).astype(jnp.float32), axis=0))
    value_total = lax.optimization_barrier(jnp.sum(lax.optimization_barrier(value_part.astype(jnp.bfloat16)).astype(jnp.float32), axis=0))
    encoded_grad = (jnp.dot(key_grad, key_weight.T, preferred_element_type=jnp.float32) + jnp.dot(value_grad, value_weight.T, preferred_element_type=jnp.float32)).astype(jnp.bfloat16)
    row_grad = encode_backward(encoded_grad, used_rows, before, inverse, enc_gain, enc_up, enc_down).reshape(STRETCHES, NLEN, DE)
    pool_grad = jnp.zeros((SLOTS, NLEN, DE), jnp.bfloat16).at[slot_seq.astype(jnp.int32)].set(row_grad)
    return (attended, query_grad, pool_grad, key_total, value_total)

def reference(queries, attended_grad, neighbour_pool, stretch_slot, enc_gain, enc_up, enc_down, key_weight, value_weight):

    def one_sequence(operands):
        return sequence_terms(operands[0], operands[1], operands[2], operands[3], enc_gain, enc_up, enc_down, key_weight, value_weight)
    attended, query_grad, pool_grad, key_totals, value_totals = lax.map(one_sequence, (queries, attended_grad, neighbour_pool, stretch_slot))
    return (attended, query_grad, pool_grad, lax.optimization_barrier(jnp.sum(key_totals, axis=0)), lax.optimization_barrier(jnp.sum(value_totals, axis=0)))
```

```python
import math

import jax
import jax.numpy as jnp
from jax import lax
from jax.experimental import pallas as pl
from jax.experimental.pallas import tpu as pltpu
from jax.sharding import PartitionSpec as P

STRETCH = 64
HD = 128
NX = 4
NZ = 8
CAP = 4
SLOTS = 64
NLEN = 128
PIECE = 16
DE = 896
FFE = 1792
HEADS = 16
WROWS = 448
WSUB = 112
TOKENS = 128
EPS = 1e-6
SCALE = 1.0 / math.sqrt(HD)

MESH = pl.DeviceIdType.MESH
BF16 = jnp.bfloat16
F32 = jnp.float32


class Place:
    def __init__(self):
        self.dp = lax.axis_index("dp")
        self.seq = lax.axis_index("seq")
        self.x = self.dp // NX
        self.y = self.dp % NX
        self.z = self.seq // 2
        self.c = self.seq % 2

    def xs(self, d):
        return (self.x + d + NX) % NX

    def ys(self, d):
        return (self.y + d + NX) % NX

    def zs(self, d):
        return (self.z + d + NZ) % NZ

    def at_x(self, d):
        return (self.xs(d) * NX + self.y, self.seq)

    def at_y(self, d):
        return (self.x * NX + self.ys(d), self.seq)

    def at_z(self, d):
        return (self.dp, self.zs(d) * 2 + self.c)

    def at_dp(self, d):
        return ((self.dp + d) % (NX * NX), self.seq)

    def sibling(self):
        return (self.dp, self.z * 2 + 1 - self.c)


def greet(partners):
    barrier = pltpu.get_barrier_semaphore()
    for partner in partners:
        pl.semaphore_signal(barrier, inc=1, device_id=partner, device_id_type=MESH)
    pl.semaphore_wait(barrier, len(partners))


class Copies:
    def __init__(self, send_sems, recv_sems):
        self.send_sems, self.recv_sems = send_sems, recv_sems
        self.count = 0
        self.all = []

    def start(self, src, dst, device):
        copy = pltpu.make_async_remote_copy(
            src_ref=src,
            dst_ref=dst,
            send_sem=self.send_sems.at[self.count],
            recv_sem=self.recv_sems.at[self.count],
            device_id=device,
            device_id_type=MESH,
        )
        self.count += 1
        self.all.append(copy)
        copy.start()
        return copy

    def finish(self):
        for copy in self.all:
            copy.wait_send()


def rows16(index):
    return pl.ds(pl.multiple_of(index * PIECE, PIECE), PIECE)


def sub(index):
    return pl.ds(pl.multiple_of(index * WSUB, 16), WSUB)


FRONT_COPIES = 56


def front_kernel(
    slot_ref, pool_ref, wk_ref, wv_ref, rows_ref, wall_ref, mid, out, ssem, rsem, lsem
):
    p = Place()
    z, c, x, y = p.z, p.c, p.x, p.y
    cp = Copies(ssem, rsem)

    def own_chunk(source):
        return pltpu.make_async_copy(
            source.at[x % 2, sub(y), :], wall_ref.at[z, c, x, sub(y), :], lsem.at[0]
        )

    @pl.when(x < 2)
    def key_chunk():
        own_chunk(wk_ref).start()

    @pl.when(x >= 2)
    def value_chunk():
        own_chunk(wv_ref).start()

    own_slots = pl.ds(p.seq * CAP, CAP)
    own_pool = pltpu.make_async_copy(pool_ref.at[:, rows16(z), :], mid.at[own_slots], lsem.at[2])
    own_pool.start()
    greet(
        [p.at_z(d) for d in range(1, NZ)]
        + [p.sibling(), p.at_x(1), p.at_x(-1), p.at_y(1), p.at_y(-1)]
    )

    own_chunk(wk_ref).wait()
    order = (4, 3, 5, 2, 6, 1, 7)

    def chunk(zz, xx, yy):
        return wall_ref.at[zz, c, xx, sub(yy), :]

    wz = [cp.start(chunk(z, x, y), chunk(z, x, y), p.at_z(d)) for d in order]
    hop1 = {
        d: cp.start(pool_ref.at[:, rows16(p.zs(d)), :], mid.at[own_slots], p.at_z(d))
        for d in order
    }
    forward = [cp.start(pool_ref.at[:, rows16(z), :], mid.at[own_slots], p.sibling())]

    for copy in wz:
        copy.wait_recv()
    lo, hi = pl.ds(0, 4), pl.ds(4, 4)

    def ring(region, first, places, at):
        src = region(first, places(0))
        return [cp.start(src, src, at(1)), cp.start(src, src, at(-1))]

    def ring2(region, first, places, at, arrived):
        arrived[0].wait_recv()
        src = region(pl.ds(first, 2), places(-1))
        one = cp.start(src, src, at(1))
        arrived[1].wait_recv()
        src = region(pl.ds(first + 2, 2), places(1))
        return [one, cp.start(src, src, at(-1))]

    def region_x(heads, xx):
        return wall_ref.at[heads, c, xx, sub(y), :]

    def region_y(heads, yy):
        return wall_ref.at[heads, c, x, sub(yy), :]

    def wide_y(heads, yy):
        return wall_ref.at[heads, c, :, sub(yy), :]

    def wide_x(heads, xx):
        return wall_ref.at[heads, c, xx, :, :]

    a1 = ring(region_x, lo, p.xs, p.at_x)
    b1 = ring(region_y, hi, p.ys, p.at_y)
    a2 = ring2(region_x, 0, p.xs, p.at_x, a1)
    b2 = ring2(region_y, 4, p.ys, p.at_y, b1)
    for copy in a2:
        copy.wait_recv()
    a3 = ring(wide_y, lo, p.ys, p.at_y)
    for copy in b2:
        copy.wait_recv()
    b3 = ring(wide_x, hi, p.xs, p.at_x)
    sib = []

    def share(src):
        sib.append(cp.start(src, src, p.sibling()))

    share(wide_y(lo, y))
    share(wide_x(hi, x))

    own_pool.wait()
    for d in (1, 7, 2, 6, 3, 5, 4):
        hop1[d].wait_recv()
        block = mid.at[pl.ds((p.zs(-d) * 2 + c) * CAP, CAP)]
        forward.append(cp.start(block, block, p.sibling()))
    for copy in forward:
        copy.wait_recv()
    hop2 = []
    for d in order + (0,):
        target = p.zs(d) * 2 + c
        for i in range(2):
            out[d, i] = mid[slot_ref[target * 2 + i]]
        dst = rows_ref.at[:, rows16(z), :]
        if d == 0:
            own_rows = pltpu.make_async_copy(out.at[d], dst, lsem.at[3])
            own_rows.start()
        else:
            hop2.append(cp.start(out.at[d], dst, p.at_z(d)))

    a4 = ring2(wide_y, 0, p.ys, p.at_y, a3)
    b4 = ring2(wide_x, 4, p.xs, p.at_x, b3)
    share(wide_y(lo, p.ys(1)))
    share(wide_y(lo, p.ys(-1)))
    share(wide_x(hi, p.xs(1)))
    share(wide_x(hi, p.xs(-1)))
    a4[0].wait_recv()
    share(wide_y(pl.ds(0, 2), p.ys(2)))
    a4[1].wait_recv()
    share(wide_y(pl.ds(2, 2), p.ys(2)))
    b4[0].wait_recv()
    share(wide_x(pl.ds(4, 2), p.xs(2)))
    b4[1].wait_recv()
    share(wide_x(pl.ds(6, 2), p.xs(2)))
    own_rows.wait()
    for copy in hop2 + sib:
        copy.wait_recv()
    cp.finish()


def front(slots, pool, wk, wv):
    anyspace = pl.BlockSpec(memory_space=pl.ANY)
    return pl.pallas_call(
        front_kernel,
        out_shape=(
            jax.ShapeDtypeStruct((2, NLEN, DE), BF16),
            jax.ShapeDtypeStruct((NZ, 2, 4, WROWS, HD), BF16),
        ),
        in_specs=[pl.BlockSpec(memory_space=pltpu.SMEM), anyspace, anyspace, anyspace],
        out_specs=(anyspace, anyspace),
        scratch_shapes=[
            pltpu.VMEM((SLOTS, PIECE, DE), BF16),
            pltpu.VMEM((NZ, 2, PIECE, DE), BF16),
            pltpu.SemaphoreType.DMA((FRONT_COPIES,)),
            pltpu.SemaphoreType.DMA((FRONT_COPIES,)),
            pltpu.SemaphoreType.DMA((4,)),
        ],
        compiler_params=pltpu.CompilerParams(
            collective_id=0, has_side_effects=True, vmem_limit_bytes=16 * 1024 * 1024
        ),
        name="front",
    )(slots, pool, wk, wv)


def dot(a, b):
    return jnp.dot(a, b, preferred_element_type=F32)


def dot_nt(a, b):
    return lax.dot_general(a, b, (((1,), (1,)), ((), ())), preferred_element_type=F32)


def dot_tn(a, b):
    return lax.dot_general(a, b, (((0,), (0,)), ((), ())), preferred_element_type=F32)


def core_kernel(
    rows_ref, gain_ref, up_ref, down_ref, w_ref, q_ref, g_ref,
    att_ref, qg_ref, pg_ref, wg_ref,
    enc_ref, enct_ref, slope_ref, inv_ref, acc_ref,
):
    head = pl.program_id(0)
    root = math.sqrt(2.0 / math.pi)
    tile = 256

    @pl.when(head == 0)
    def encode():
        rows = rows_ref[...].astype(F32)
        inverse = lax.rsqrt(jnp.mean(rows * rows, axis=-1, keepdims=True) + EPS)
        inv_ref[...] = inverse
        normed = (rows * inverse * gain_ref[...]).astype(BF16)
        total = rows
        for t in range(FFE // tile):
            span = slice(t * tile, (t + 1) * tile)
            before = dot(normed, up_ref[:, span])
            square = before * before
            th = jnp.tanh(root * before * (1.0 + 0.044715 * square))
            half = 0.5 * (1.0 + th)
            slope_ref[:, span] = half + 0.5 * before * (1.0 - th * th) * root * (
                1.0 + 3.0 * 0.044715 * square
            )
            total = total + dot((before * half).astype(BF16), down_ref[span, :])
        encoded = total.astype(BF16)
        enc_ref[...] = encoded
        enct_ref[...] = encoded.T
        acc_ref[...] = jnp.zeros_like(acc_ref)

    w = jnp.concatenate([w_ref[0, 0], w_ref[0, 1]], axis=1)
    kv = dot(enc_ref[...], w).astype(BF16)
    kv_grads = []
    for i in range(2):
        tokens = slice(i * STRETCH, (i + 1) * STRETCH)
        k = kv[i * NLEN : (i + 1) * NLEN, :HD]
        v = kv[i * NLEN : (i + 1) * NLEN, HD:]
        q, g = q_ref[tokens, :], g_ref[tokens, :]
        exponent = jnp.exp(dot_nt(q, k) * SCALE)
        weights = exponent / jnp.sum(exponent, axis=-1, keepdims=True)
        probs = weights.astype(BF16)
        att_ref[tokens, :] = dot(probs, v).astype(BF16)
        prob_grad = dot_nt(g, v)
        mean = jnp.sum(weights * prob_grad, axis=-1, keepdims=True)
        score_grad = (weights * (prob_grad - mean) * SCALE).astype(BF16)
        qg_ref[tokens, :] = dot(score_grad, k).astype(BF16)
        kv_grads.append(
            jnp.concatenate([dot_tn(score_grad, q), dot_tn(probs, g)], axis=1).astype(BF16)
        )
    kv_grad = jnp.concatenate(kv_grads, axis=0)
    part = dot(enct_ref[...], kv_grad).astype(BF16)
    wg_ref[0, 0] = part[:, :HD]
    wg_ref[0, 1] = part[:, HD:]
    acc_ref[...] += dot_nt(kv_grad, w)

    @pl.when(head == HEADS - 1)
    def encode_back():
        encoded_grad = acc_ref[...].astype(BF16)
        normed_grad = jnp.zeros((2 * NLEN, DE), F32)
        for t in range(FFE // tile):
            span = slice(t * tile, (t + 1) * tile)
            before_grad = (dot_nt(encoded_grad, down_ref[span, :]) * slope_ref[:, span]).astype(BF16)
            normed_grad = normed_grad + dot_nt(before_grad, up_ref[:, span])
        rows = rows_ref[...].astype(F32)
        inverse = inv_ref[...]
        scaled = gain_ref[...] * normed_grad
        result = (
            encoded_grad.astype(F32)
            + inverse * scaled
            - rows
            * (inverse * inverse * inverse)
            * jnp.mean(rows * scaled, axis=-1, keepdims=True)
        )
        pg_ref[...] = result.astype(BF16)


def core(rows, gain, up, down, wall, queries, grads):
    whole = pl.BlockSpec(memory_space=pltpu.VMEM)
    column = pl.BlockSpec((TOKENS, HD), lambda h: (0, h))
    block = pl.BlockSpec((1, 2, DE, HD), lambda h: (h, 0, 0, 0))
    r = 2 * NLEN
    return pl.pallas_call(
        core_kernel,
        grid=(HEADS,),
        out_shape=(
            jax.ShapeDtypeStruct((TOKENS, HEADS * HD), BF16),
            jax.ShapeDtypeStruct((TOKENS, HEADS * HD), BF16),
            jax.ShapeDtypeStruct((r, DE), BF16),
            jax.ShapeDtypeStruct((HEADS, 2, DE, HD), BF16),
        ),
        in_specs=[whole, whole, whole, whole, block, column, column],
        out_specs=(column, column, pl.BlockSpec((r, DE), lambda h: (0, 0)), block),
        scratch_shapes=[
            pltpu.VMEM((r, DE), BF16),
            pltpu.VMEM((DE, r), BF16),
            pltpu.VMEM((r, FFE), F32),
            pltpu.VMEM((r, 1), F32),
            pltpu.VMEM((r, DE), F32),
        ],
        compiler_params=pltpu.CompilerParams(
            dimension_semantics=("arbitrary",), vmem_limit_bytes=48 * 1024 * 1024
        ),
        name="core",
    )(rows, gain, up, down, wall, queries, grads)


BACK_COPIES = 72


def back_kernel(
    user_ref, pg_ref, wg_ref, pool_ref, kw_ref, vw_ref,
    part, other, mid, out, ya1, ya2, xa1, xa2, xb1, xb2, yb1, yb2, zbuf, fin, ssem, rsem, lsem,
):
    p = Place()
    z, c, x, y = p.z, p.c, p.x, p.y
    cp = Copies(ssem, rsem)
    own_two = pl.ds(p.seq * 2 + 1, 2)
    own_mid = pltpu.make_async_copy(pg_ref.at[:, rows16(z), :], mid.at[own_two], lsem.at[0])
    own_mid.start()
    own_part = pltpu.make_async_copy(wg_ref.at[:, c], part, lsem.at[1])
    own_part.start()
    greet(
        [p.at_z(d) for d in range(1, NZ)] + [p.sibling()] + [p.at_dp(d) for d in range(1, NX * NX)]
    )
    order = (4, 3, 5, 2, 6, 1, 7)
    forward = [cp.start(pg_ref.at[:, rows16(z), :], mid.at[own_two], p.sibling())]
    hop1 = {
        d: cp.start(pg_ref.at[:, rows16(p.zs(d)), :], mid.at[own_two], p.at_z(d)) for d in order
    }
    sib = [cp.start(wg_ref.at[h, 1 - c], other.at[h], p.sibling()) for h in range(NZ)]
    mid[0] = jnp.zeros((PIECE, DE), BF16)
    own_part.wait()

    def add_sibling(h):
        sib[h].wait_recv()

        def body(i, carry):
            part[h, i] = (part[h, i].astype(F32) + other[h, i].astype(F32)).astype(BF16)
            return carry

        lax.fori_loop(0, 4, body, 0)

    def wide_y(first, count, yy):
        return part.at[pl.ds(first, count), :, sub(yy), :]

    def wide_x(first, count, xx):
        return part.at[pl.ds(first, count), xx, :, :]

    def region_x(first, count, xx):
        return part.at[pl.ds(first, count), xx, sub(y), :]

    def region_y(first, count, yy):
        return part.at[pl.ds(first, count), x, sub(yy), :]

    def far(region, first, places, at, land):
        return [
            cp.start(region(first, 2, places(2)), land.at[0], at(1)),
            cp.start(region(first + 2, 2, places(2)), land.at[1], at(-1)),
        ]

    def near(region, first, places, at, arrived, land1, land2):
        sent = []
        for side, d in ((0, 1), (1, -1)):
            arrived[side].wait_recv()
            block = region(first + 2 * side, 2, places(d))
            block[...] = (block[...].astype(F32) + land1[side].astype(F32)).astype(BF16)
            sent.append(cp.start(region(first, 4, places(d)), land2.at[side], at(d)))
        return sent

    def close(region, first, places, arrived, land2):
        for copy in arrived:
            copy.wait_recv()
        block = region(first, 4, places(0))
        block[...] = (
            block[...].astype(F32) + land2[0].astype(F32) + land2[1].astype(F32)
        ).astype(BF16)

    for h in range(4):
        add_sibling(h)
    a1 = far(wide_y, 0, p.ys, p.at_y, ya1)
    for h in range(4, NZ):
        add_sibling(h)
    b1 = far(wide_x, 4, p.xs, p.at_x, xb1)

    for d in (1, 7, 2, 6, 3, 5, 4):
        hop1[d].wait_recv()
        block = mid.at[pl.ds((p.zs(-d) * 2 + c) * 2 + 1, 2)]
        forward.append(cp.start(block, block, p.sibling()))
    a2 = near(wide_y, 0, p.ys, p.at_y, a1, ya1, ya2)
    b2 = near(wide_x, 4, p.xs, p.at_x, b1, xb1, xb2)
    own_mid.wait()
    for copy in forward:
        copy.wait_recv()
    hop2 = []
    for d in order + (0,):
        target = p.zs(d) * 2 + c
        for j in range(CAP):
            out[d, j] = mid[user_ref[target * CAP + j]]
        dst = pool_ref.at[:, rows16(z), :]
        if d == 0:
            own_rows = pltpu.make_async_copy(out.at[d], dst, lsem.at[2])
            own_rows.start()
        else:
            hop2.append(cp.start(out.at[d], dst, p.at_z(d)))

    close(wide_y, 0, p.ys, a2, ya2)
    a3 = far(region_x, 0, p.xs, p.at_x, xa1)
    close(wide_x, 4, p.xs, b2, xb2)
    b3 = far(region_y, 4, p.ys, p.at_y, yb1)
    a4 = near(region_x, 0, p.xs, p.at_x, a3, xa1, xa2)
    b4 = near(region_y, 4, p.ys, p.at_y, b3, yb1, yb2)
    close(region_x, 0, p.xs, a4, xa2)
    close(region_y, 4, p.ys, b4, yb2)
    zsum = [cp.start(part.at[p.zs(d), x, sub(y), :], zbuf.at[d], p.at_z(d)) for d in order]
    for copy in zsum:
        copy.wait_recv()
    total = part[z, x, sub(y), :].astype(F32)
    for d in range(1, NZ):
        total = total + zbuf[d].astype(F32)
    fin[x, y] = total.astype(BF16)
    last = [cp.start(fin.at[x, y], fin.at[x, y], p.at_dp(d)) for d in range(1, NX * NX)]
    for copy in last:
        copy.wait_recv()
    for xx in range(2):
        for yy in range(NX):
            span = slice(xx * WROWS + yy * WSUB, xx * WROWS + (yy + 1) * WSUB)
            kw_ref[span, :] = fin[xx, yy].astype(F32)
            vw_ref[span, :] = fin[xx + 2, yy].astype(F32)
    own_rows.wait()
    for copy in hop2:
        copy.wait_recv()
    cp.finish()


def back(user, pool_rows, wgrads):
    anyspace = pl.BlockSpec(memory_space=pl.ANY)
    whole = pl.BlockSpec(memory_space=pltpu.VMEM)
    return pl.pallas_call(
        back_kernel,
        out_shape=(
            jax.ShapeDtypeStruct((CAP, NLEN, DE), BF16),
            jax.ShapeDtypeStruct((DE, HD), F32),
            jax.ShapeDtypeStruct((DE, HD), F32),
        ),
        in_specs=[pl.BlockSpec(memory_space=pltpu.SMEM), anyspace, anyspace],
        out_specs=(anyspace, whole, whole),
        scratch_shapes=[
            pltpu.VMEM((NZ, 4, WROWS, HD), BF16),
            pltpu.VMEM((NZ, 4, WROWS, HD), BF16),
            pltpu.VMEM((1 + SLOTS // 2, PIECE, DE), BF16),
            pltpu.VMEM((NZ, CAP, PIECE, DE), BF16),
            pltpu.VMEM((2, 2, 4, WSUB, HD), BF16),
            pltpu.VMEM((2, 4, 4, WSUB, HD), BF16),
            pltpu.VMEM((2, 2, WSUB, HD), BF16),
            pltpu.VMEM((2, 4, WSUB, HD), BF16),
            pltpu.VMEM((2, 2, WROWS, HD), BF16),
            pltpu.VMEM((2, 4, WROWS, HD), BF16),
            pltpu.VMEM((2, 2, WSUB, HD), BF16),
            pltpu.VMEM((2, 4, WSUB, HD), BF16),
            pltpu.VMEM((NZ, WSUB, HD), BF16),
            pltpu.VMEM((NX, NX, WSUB, HD), BF16),
            pltpu.SemaphoreType.DMA((BACK_COPIES,)),
            pltpu.SemaphoreType.DMA((BACK_COPIES,)),
            pltpu.SemaphoreType.DMA((3,)),
        ],
        compiler_params=pltpu.CompilerParams(
            collective_id=1, has_side_effects=True, vmem_limit_bytes=32 * 1024 * 1024
        ),
        name="back",
    )(user, pool_rows, wgrads)


def on_device(queries, attended_grad, pool, stretch_slot, gain, up, down, key_w, value_w):
    slots = stretch_slot[0]
    match = slots[:, None] == jnp.arange(SLOTS, dtype=jnp.int32)[None, :]
    place = jnp.arange(1, slots.shape[0] + 1, dtype=jnp.int32)[:, None]
    user = jnp.sum(jnp.where(match, place, 0), axis=0)
    rows, wall = front(slots, pool[0], key_w.reshape(2, WROWS, HD), value_w.reshape(2, WROWS, HD))
    attended, query_grad, pool_rows, wgrads = core(
        rows.reshape(2 * NLEN, DE),
        gain.reshape(1, DE),
        up,
        down,
        wall.reshape(HEADS, 2, DE, HD),
        queries[0],
        attended_grad[0],
    )
    pool_grad, key_grad, value_grad = back(
        user, pool_rows.reshape(2, NLEN, DE), wgrads.reshape(NZ, 2, 4, WROWS, HD)
    )
    return attended[None], query_grad[None], pool_grad[None], key_grad, value_grad


def solution(mesh):
    return jax.shard_map(
        on_device,
        mesh=mesh,
        in_specs=(
            P("dp", "seq", None),
            P("dp", "seq", None),
            P("dp", "seq", None, None),
            P("dp", None),
            P(),
            P(),
            P(),
            P(None, "seq"),
            P(None, "seq"),
        ),
        out_specs=(
            P("dp", "seq", None),
            P("dp", "seq", None),
            P("dp", "seq", None, None),
            P(None, "seq"),
            P(None, "seq"),
        ),
        check_vma=False,
    )
```

```python
import math

import jax
import jax.numpy as jnp
from jax import lax
from jax.experimental import pallas as pl
from jax.experimental.pallas import tpu as pltpu
from jax.sharding import PartitionSpec as P

STRETCH = 64
HD = 128
NX = 4
NZ = 8
CAP = 4
SLOTS = 64
NLEN = 128
PIECE = 16
DE = 896
FFE = 1792
HEADS = 16
WROWS = 448
WSUB = 112
TOKENS = 128
EPS = 1e-6
SCALE = 1.0 / math.sqrt(HD)

MESH = pl.DeviceIdType.MESH
BF16 = jnp.bfloat16
F32 = jnp.float32


class Place:
    def __init__(self):
        self.dp = lax.axis_index("dp")
        self.seq = lax.axis_index("seq")
        self.x = self.dp // NX
        self.y = self.dp % NX
        self.z = self.seq // 2
        self.c = self.seq % 2

    def xs(self, d):
        return (self.x + d + NX) % NX

    def ys(self, d):
        return (self.y + d + NX) % NX

    def zs(self, d):
        return (self.z + d + NZ) % NZ

    def at_x(self, d):
        return (self.xs(d) * NX + self.y, self.seq)

    def at_y(self, d):
        return (self.x * NX + self.ys(d), self.seq)

    def at_z(self, d):
        return (self.dp, self.zs(d) * 2 + self.c)

    def at_dp(self, d):
        return ((self.dp + d) % (NX * NX), self.seq)

    def sibling(self):
        return (self.dp, self.z * 2 + 1 - self.c)


def greet(partners):
    barrier = pltpu.get_barrier_semaphore()
    for partner in partners:
        pl.semaphore_signal(barrier, inc=1, device_id=partner, device_id_type=MESH)
    pl.semaphore_wait(barrier, len(partners))


class Copies:
    def __init__(self, send_sems, recv_sems):
        self.send_sems, self.recv_sems = send_sems, recv_sems
        self.count = 0
        self.all = []

    def start(self, src, dst, device):
        copy = pltpu.make_async_remote_copy(
            src_ref=src,
            dst_ref=dst,
            send_sem=self.send_sems.at[self.count],
            recv_sem=self.recv_sems.at[self.count],
            device_id=device,
            device_id_type=MESH,
        )
        self.count += 1
        self.all.append(copy)
        copy.start()
        return copy

    def finish(self):
        for copy in self.all:
            copy.wait_send()


def rows16(index):
    return pl.ds(pl.multiple_of(index * PIECE, PIECE), PIECE)


def sub(index):
    return pl.ds(pl.multiple_of(index * WSUB, 16), WSUB)


COPIES = 136
GROUP = 8
TILE = 256
ROWS = 2 * NLEN


def dot(a, b):
    return jnp.dot(a, b, preferred_element_type=F32)


def dot_nt(a, b):
    return lax.dot_general(a, b, (((1,), (1,)), ((), ())), preferred_element_type=F32)


def dot_tn(a, b):
    return lax.dot_general(a, b, (((0,), (0,)), ((), ())), preferred_element_type=F32)


def encode(rows_ref, gain_ref, up, down, slope, inv):
    rows = rows_ref[...].reshape(ROWS, DE).astype(F32)
    inverse = lax.rsqrt(jnp.mean(rows * rows, axis=-1, keepdims=True) + EPS)
    inv[...] = inverse
    normed = (rows * inverse * gain_ref[...]).astype(BF16)
    root = math.sqrt(2.0 / math.pi)
    before = dot(normed, up[...])
    square = before * before
    th = jnp.tanh(root * before * (1.0 + 0.044715 * square))
    half = 0.5 * (1.0 + th)
    slope[...] = half + 0.5 * before * (1.0 - th * th) * root * (1.0 + 3.0 * 0.044715 * square)
    return (rows + dot((before * half).astype(BF16), down[...])).astype(BF16)


def encode_back(encoded_grad, rows_ref, gain_ref, up, down, slope, inv):
    before_grad = (dot_nt(encoded_grad, down[...]) * slope[...]).astype(BF16)
    normed_grad = dot_nt(before_grad, up[...])
    rows = rows_ref[...].reshape(ROWS, DE).astype(F32)
    inverse = inv[...]
    scaled = gain_ref[...] * normed_grad
    result = (
        encoded_grad.astype(F32)
        + inverse * scaled
        - rows
        * (inverse * inverse * inverse)
        * jnp.mean(rows * scaled, axis=-1, keepdims=True)
    )
    return result.astype(BF16)


def attention(first, count, q_all, g_all, kv, kvg, att, qg):
    zero = jnp.zeros((STRETCH, HD), BF16)
    units = [(h, i) for h in range(first, first + count) for i in range(2)]
    pairs, products, mixes = [], [], []
    for h, i in units:
        column, tokens = slice(h * HD, (h + 1) * HD), slice(i * STRETCH, (i + 1) * STRETCH)
        pair = jnp.concatenate(
            [
                jnp.concatenate([q_all[tokens, column], zero], axis=1),
                jnp.concatenate([zero, g_all[tokens, column]], axis=1),
            ],
            axis=0,
        )
        pairs.append(pair)
        products.append(dot_nt(pair, kv[h // 2, h % 2, i * NLEN : (i + 1) * NLEN, :]))
    for product in products:
        exponent = jnp.exp(product[:STRETCH] * SCALE)
        weights = exponent / jnp.sum(exponent, axis=-1, keepdims=True)
        prob_grad = product[STRETCH:]
        mean = jnp.sum(weights * prob_grad, axis=-1, keepdims=True)
        score_grad = weights * (prob_grad - mean) * SCALE
        mixes.append(jnp.concatenate([score_grad, weights], axis=0).astype(BF16))
    for (h, i), pair, mix in zip(units, pairs, mixes):
        column, tokens = slice(h * HD, (h + 1) * HD), slice(i * STRETCH, (i + 1) * STRETCH)
        keys = slice(i * NLEN, (i + 1) * NLEN)
        o = dot(mix, kv[h // 2, h % 2, keys, :])
        qg[tokens, column] = o[:STRETCH, :HD].astype(BF16)
        att[tokens, column] = o[STRETCH:, HD:].astype(BF16)
        kvg[h // 2, h % 2, keys, :] = dot_tn(mix, pair).astype(BF16)


def whole_kernel(
    slot_ref, gain_ref, pool_ref, wk_ref, wv_ref, up_ref, down_ref, q_ref, g_ref,
    att_ref, qg_ref, pg_ref, kw_ref, vw_ref,
    user, mid, out, rows, wall, up, down, q_all, g_all, att, qg, slope, inv, enc, enc_other,
    enct, kv, kvg, kvg_other, part, pg, mid2, out2, ya1, ya2, xa1, xa2, xb1, xb2, yb1, yb2,
    zbuf, fin, ssem, rsem, lsem,
):
    p = Place()
    z, c, x, y = p.z, p.c, p.x, p.y
    cp = Copies(ssem, rsem)

    def local(src, dst, index):
        return pltpu.make_async_copy(src, dst, lsem.at[index])

    def own_chunk(source):
        return local(source.at[x % 2, sub(y), :], wall.at[z, c, x, sub(y), :], 0)

    @pl.when(x < 2)
    def key_chunk():
        own_chunk(wk_ref).start()

    @pl.when(x >= 2)
    def value_chunk():
        own_chunk(wv_ref).start()

    own_slots = pl.ds(p.seq * CAP, CAP)
    own_pool = local(pool_ref.at[:, rows16(z), :], mid.at[own_slots], 1)
    own_pool.start()
    loads = [
        local(src, dst, 2 + n)
        for n, (src, dst) in enumerate(
            ((up_ref, up), (down_ref, down), (q_ref, q_all), (g_ref, g_all))
        )
    ]
    for load in loads:
        load.start()
    greet(
        [p.at_z(d) for d in range(1, NZ)] + [p.sibling()] + [p.at_dp(d) for d in range(1, NX * NX)]
    )

    own_chunk(wk_ref).wait()
    order = (4, 3, 5, 2, 6, 1, 7)

    def chunk(zz, xx, yy):
        return wall.at[zz, c, xx, sub(yy), :]

    wz = [cp.start(chunk(z, x, y), chunk(z, x, y), p.at_z(d)) for d in order]
    hop1 = {
        d: cp.start(pool_ref.at[:, rows16(p.zs(d)), :], mid.at[own_slots], p.at_z(d))
        for d in order
    }
    forward = [cp.start(pool_ref.at[:, rows16(z), :], mid.at[own_slots], p.sibling())]

    for copy in wz:
        copy.wait_recv()
    lo, hi = pl.ds(0, 4), pl.ds(4, 4)

    def ring(region, heads, places, at):
        src = region(heads, places(0))
        return [cp.start(src, src, at(1)), cp.start(src, src, at(-1))]

    def ring2(region, first, places, at, arrived):
        arrived[0].wait_recv()
        src = region(pl.ds(first, 2), places(-1))
        one = cp.start(src, src, at(1))
        arrived[1].wait_recv()
        src = region(pl.ds(first + 2, 2), places(1))
        return [one, cp.start(src, src, at(-1))]

    def row_x(heads, xx):
        return wall.at[heads, c, xx, sub(y), :]

    def row_y(heads, yy):
        return wall.at[heads, c, x, sub(yy), :]

    def wide_y(heads, yy):
        return wall.at[heads, c, :, sub(yy), :]

    def wide_x(heads, xx):
        return wall.at[heads, c, xx, :, :]

    sib = []

    def share(src):
        sib.append(cp.start(src, src, p.sibling()))

    def hand(distances):
        for d in distances:
            hop1[d].wait_recv()
            block = mid.at[pl.ds((p.zs(-d) * 2 + c) * CAP, CAP)]
            forward.append(cp.start(block, block, p.sibling()))

    a1 = ring(row_x, lo, p.xs, p.at_x)
    b1 = ring(row_y, hi, p.ys, p.at_y)
    a2 = ring2(row_x, 0, p.xs, p.at_x, a1)
    b2 = ring2(row_y, 4, p.ys, p.at_y, b1)
    for copy in a2:
        copy.wait_recv()
    a3 = ring(wide_y, lo, p.ys, p.at_y)
    for copy in b2:
        copy.wait_recv()
    b3 = ring(wide_x, hi, p.xs, p.at_x)
    share(wide_y(lo, y))
    share(wide_x(hi, x))
    own_pool.wait()
    hand((1, 7, 2, 6))

    def find_user(k, carry):
        slot = (p.zs(k // CAP) * 2 + c) * CAP + k % CAP
        found = jnp.int32(0)
        for stretch in range(SLOTS // 2):
            found = jnp.where(slot_ref[stretch] == slot, stretch + 1, found)
        user[k] = found
        return carry

    lax.fori_loop(0, NZ * CAP, find_user, 0)
    hand((3, 5, 4))
    for copy in forward:
        copy.wait_recv()
    hop2 = []
    for d in order + (0,):
        target = p.zs(d) * 2 + c
        for i in range(2):
            out[d, i] = mid[slot_ref[target * 2 + i]]
        dst = rows.at[:, rows16(z), :]
        if d == 0:
            own_rows = local(out.at[d], dst, 6)
            own_rows.start()
        else:
            hop2.append(cp.start(out.at[d], dst, p.at_z(d)))

    a4 = ring2(wide_y, 0, p.ys, p.at_y, a3)
    b4 = ring2(wide_x, 4, p.xs, p.at_x, b3)
    for d in (1, -1):
        share(wide_y(lo, p.ys(d)))
        share(wide_x(hi, p.xs(d)))
    for side in range(2):
        a4[side].wait_recv()
        share(wide_y(pl.ds(2 * side, 2), p.ys(2)))
        b4[side].wait_recv()
        share(wide_x(pl.ds(4 + 2 * side, 2), p.xs(2)))
    own_rows.wait()
    for copy in hop2:
        copy.wait_recv()

    for load in loads:
        load.wait()
    encoded = encode(rows, gain_ref, up, down, slope, inv)
    enc[...] = encoded
    enc_sent = cp.start(enc, enc_other, p.sibling())
    enct[:, :ROWS] = encoded.T
    for copy in sib:
        copy.wait_recv()

    def both(h):
        k = wall[h // 2, h % 2, pl.ds(0, 2)].reshape(DE, HD)
        v = wall[h // 2, h % 2, pl.ds(2, 2)].reshape(DE, HD)
        return jnp.concatenate([k, v], axis=1)

    kvg_sent = []
    for first in range(0, HEADS, GROUP):
        for h in range(first, first + GROUP):
            kv[h // 2, h % 2] = dot(enc[...], both(h)).astype(BF16)
        attention(first, GROUP, q_all, g_all, kv, kvg, att, qg)
        span = pl.ds(first // 2, GROUP // 2)
        kvg_sent.append(cp.start(kvg.at[span, 1 - c], kvg_other.at[span], p.sibling()))
    results = [local(att, att_ref, 7), local(qg, qg_ref, 8)]
    for result in results:
        result.start()
    total = jnp.zeros((ROWS, DE), F32)
    for h in range(HEADS):
        total = total + dot_nt(kvg[h // 2, h % 2], both(h))
    pg[...] = encode_back(
        total.astype(BF16), rows, gain_ref, up, down, slope, inv
    ).reshape(2, NLEN, DE)

    own_two = pl.ds(p.seq * 2 + 1, 2)
    own_mid = local(pg.at[:, rows16(z), :], mid2.at[own_two], 9)
    own_mid.start()
    back1 = {
        d: cp.start(pg.at[:, rows16(p.zs(d)), :], mid2.at[own_two], p.at_z(d)) for d in order
    }
    returns = [cp.start(pg.at[:, rows16(z), :], mid2.at[own_two], p.sibling())]
    mid2[0] = jnp.zeros((PIECE, DE), BF16)

    enc_sent.wait_recv()
    enct[:, ROWS:] = enc_other[...].T

    def weight_grad(h):
        grads = jnp.concatenate([kvg[h, c], kvg_other[h]], axis=0)
        block = dot(enct[...], grads).astype(BF16)
        for n in range(4):
            part[h, n] = block[(n % 2) * WROWS : (n % 2 + 1) * WROWS, (n // 2) * HD : (n // 2 + 1) * HD]

    def sum_y(first, count, yy):
        return part.at[pl.ds(first, count), :, sub(yy), :]

    def sum_x(first, count, xx):
        return part.at[pl.ds(first, count), xx, :, :]

    def narrow_x(first, count, xx):
        return part.at[pl.ds(first, count), xx, sub(y), :]

    def narrow_y(first, count, yy):
        return part.at[pl.ds(first, count), x, sub(yy), :]

    def far(region, first, places, at, land):
        return [
            cp.start(region(first, 2, places(2)), land.at[0], at(1)),
            cp.start(region(first + 2, 2, places(2)), land.at[1], at(-1)),
        ]

    def near(region, first, places, at, arrived, land1, land2):
        sent = []
        for side, d in ((0, 1), (1, -1)):
            arrived[side].wait_recv()
            block = region(first + 2 * side, 2, places(d))
            block[...] = (block[...].astype(F32) + land1[side].astype(F32)).astype(BF16)
            sent.append(cp.start(region(first, 4, places(d)), land2.at[side], at(d)))
        return sent

    def close(region, first, places, arrived, land2):
        for copy in arrived:
            copy.wait_recv()
        block = region(first, 4, places(0))
        block[...] = (
            block[...].astype(F32) + land2[0].astype(F32) + land2[1].astype(F32)
        ).astype(BF16)

    kvg_sent[0].wait_recv()
    for h in range(4):
        weight_grad(h)
    a1 = far(sum_y, 0, p.ys, p.at_y, ya1)
    kvg_sent[1].wait_recv()
    for h in range(4, NZ):
        weight_grad(h)
    b1 = far(sum_x, 4, p.xs, p.at_x, xb1)

    def give(distances):
        for d in distances:
            back1[d].wait_recv()
            block = mid2.at[pl.ds((p.zs(-d) * 2 + c) * 2 + 1, 2)]
            returns.append(cp.start(block, block, p.sibling()))

    give((1, 7, 2, 6))
    a2 = near(sum_y, 0, p.ys, p.at_y, a1, ya1, ya2)
    b2 = near(sum_x, 4, p.xs, p.at_x, b1, xb1, xb2)
    give((3, 5, 4))
    own_mid.wait()
    for copy in returns:
        copy.wait_recv()
    back2 = []
    for d in order + (0,):
        for j in range(CAP):
            out2[d, j] = mid2[user[d * CAP + j]]
        dst = pg_ref.at[:, rows16(z), :]
        if d == 0:
            own_back = local(out2.at[d], dst, 10)
            own_back.start()
        else:
            back2.append(cp.start(out2.at[d], dst, p.at_z(d)))

    close(sum_y, 0, p.ys, a2, ya2)
    a3 = far(narrow_x, 0, p.xs, p.at_x, xa1)
    close(sum_x, 4, p.xs, b2, xb2)
    b3 = far(narrow_y, 4, p.ys, p.at_y, yb1)
    a4 = near(narrow_x, 0, p.xs, p.at_x, a3, xa1, xa2)
    b4 = near(narrow_y, 4, p.ys, p.at_y, b3, yb1, yb2)
    close(narrow_x, 0, p.xs, a4, xa2)
    close(narrow_y, 4, p.ys, b4, yb2)
    zsum = [cp.start(part.at[p.zs(d), x, sub(y), :], zbuf.at[d], p.at_z(d)) for d in order]
    for copy in zsum:
        copy.wait_recv()
    total = part[z, x, sub(y), :].astype(F32)
    for d in range(1, NZ):
        total = total + zbuf[d].astype(F32)
    fin[x, y] = total.astype(BF16)
    last = [cp.start(fin.at[x, y], fin.at[x, y], p.at_dp(d)) for d in range(1, NX * NX)]
    for copy in last:
        copy.wait_recv()
    for xx in range(2):
        for yy in range(NX):
            span = slice(xx * WROWS + yy * WSUB, xx * WROWS + (yy + 1) * WSUB)
            kw_ref[span, :] = fin[xx, yy].astype(F32)
            vw_ref[span, :] = fin[xx + 2, yy].astype(F32)
    own_back.wait()
    for result in results:
        result.wait()
    for copy in back2:
        copy.wait_recv()
    cp.finish()


def whole(slots, gain, pool, wk, wv, up, down, queries, grads):
    anyspace = pl.BlockSpec(memory_space=pl.ANY)
    vmem = pl.BlockSpec(memory_space=pltpu.VMEM)
    width = HEADS * HD

    def scratch(*shape):
        return pltpu.VMEM(shape, BF16)

    return pl.pallas_call(
        whole_kernel,
        out_shape=(
            jax.ShapeDtypeStruct((TOKENS, width), BF16),
            jax.ShapeDtypeStruct((TOKENS, width), BF16),
            jax.ShapeDtypeStruct((CAP, NLEN, DE), BF16),
            jax.ShapeDtypeStruct((DE, HD), F32),
            jax.ShapeDtypeStruct((DE, HD), F32),
        ),
        in_specs=[pl.BlockSpec(memory_space=pltpu.SMEM), vmem] + [anyspace] * 7,
        out_specs=(anyspace, anyspace, anyspace, vmem, vmem),
        scratch_shapes=[
            pltpu.SMEM((NZ * CAP,), jnp.int32),
            scratch(SLOTS, PIECE, DE),
            scratch(NZ, 2, PIECE, DE),
            scratch(2, NLEN, DE),
            scratch(NZ, 2, 4, WROWS, HD),
            scratch(DE, FFE),
            scratch(FFE, DE),
            scratch(TOKENS, width),
            scratch(TOKENS, width),
            scratch(TOKENS, width),
            scratch(TOKENS, width),
            pltpu.VMEM((ROWS, FFE), F32),
            pltpu.VMEM((ROWS, 1), F32),
            scratch(ROWS, DE),
            scratch(ROWS, DE),
            scratch(DE, 2 * ROWS),
            scratch(NZ, 2, ROWS, 2 * HD),
            scratch(NZ, 2, ROWS, 2 * HD),
            scratch(NZ, ROWS, 2 * HD),
            scratch(NZ, 4, WROWS, HD),
            scratch(2, NLEN, DE),
            scratch(1 + SLOTS // 2, PIECE, DE),
            scratch(NZ, CAP, PIECE, DE),
            scratch(2, 2, 4, WSUB, HD),
            scratch(2, 4, 4, WSUB, HD),
            scratch(2, 2, WSUB, HD),
            scratch(2, 4, WSUB, HD),
            scratch(2, 2, WROWS, HD),
            scratch(2, 4, WROWS, HD),
            scratch(2, 2, WSUB, HD),
            scratch(2, 4, WSUB, HD),
            scratch(NZ, WSUB, HD),
            scratch(NX, NX, WSUB, HD),
            pltpu.SemaphoreType.DMA((COPIES,)),
            pltpu.SemaphoreType.DMA((COPIES,)),
            pltpu.SemaphoreType.DMA((11,)),
        ],
        compiler_params=pltpu.CompilerParams(
            collective_id=0, has_side_effects=True, vmem_limit_bytes=56 * 1024 * 1024
        ),
        name="whole",
    )(slots, gain, pool, wk, wv, up, down, queries, grads)


def on_device(queries, attended_grad, pool, stretch_slot, gain, up, down, key_w, value_w):
    attended, query_grad, pool_grad, key_grad, value_grad = whole(
        stretch_slot[0],
        gain.reshape(1, DE),
        pool[0],
        key_w.reshape(2, WROWS, HD),
        value_w.reshape(2, WROWS, HD),
        up,
        down,
        queries[0],
        attended_grad[0],
    )
    return attended[None], query_grad[None], pool_grad[None], key_grad, value_grad


def solution(mesh):
    return jax.shard_map(
        on_device,
        mesh=mesh,
        in_specs=(
            P("dp", "seq", None),
            P("dp", "seq", None),
            P("dp", "seq", None, None),
            P("dp", None),
            P(),
            P(),
            P(),
            P(None, "seq"),
            P(None, "seq"),
        ),
        out_specs=(
            P("dp", "seq", None),
            P("dp", "seq", None),
            P("dp", "seq", None, None),
            P(None, "seq"),
            P(None, "seq"),
        ),
        check_vma=False,
    )
```

```python
import math

import jax
import jax.numpy as jnp
from jax import lax
from jax.experimental import pallas as pl
from jax.experimental.pallas import tpu as pltpu
from jax.sharding import PartitionSpec as P

STRETCH = 64
HD = 128
NX = 4
NZ = 8
CAP = 4
SLOTS = 64
NLEN = 128
PIECE = 16
DE = 896
FFE = 1792
HEADS = 16
WROWS = 448
WSUB = 112
TOKENS = 128
EPS = 1e-6
SCALE = 1.0 / math.sqrt(HD)

MESH = pl.DeviceIdType.MESH
BF16 = jnp.bfloat16
F32 = jnp.float32


class Place:
    def __init__(self):
        self.dp = lax.axis_index("dp")
        self.seq = lax.axis_index("seq")
        self.x = self.dp // NX
        self.y = self.dp % NX
        self.z = self.seq // 2
        self.c = self.seq % 2

    def xs(self, d):
        return (self.x + d + NX) % NX

    def ys(self, d):
        return (self.y + d + NX) % NX

    def zs(self, d):
        return (self.z + d + NZ) % NZ

    def at_x(self, d):
        return (self.xs(d) * NX + self.y, self.seq)

    def at_y(self, d):
        return (self.x * NX + self.ys(d), self.seq)

    def at_z(self, d):
        return (self.dp, self.zs(d) * 2 + self.c)

    def at_dp(self, d):
        return ((self.dp + d) % (NX * NX), self.seq)

    def sibling(self):
        return (self.dp, self.z * 2 + 1 - self.c)


def greet(partners):
    barrier = pltpu.get_barrier_semaphore()
    for partner in partners:
        pl.semaphore_signal(barrier, inc=1, device_id=partner, device_id_type=MESH)
    pl.semaphore_wait(barrier, len(partners))


class Copies:
    def __init__(self, send_sems, recv_sems):
        self.send_sems, self.recv_sems = send_sems, recv_sems
        self.count = 0
        self.all = []

    def start(self, src, dst, device):
        copy = pltpu.make_async_remote_copy(
            src_ref=src,
            dst_ref=dst,
            send_sem=self.send_sems.at[self.count],
            recv_sem=self.recv_sems.at[self.count],
            device_id=device,
            device_id_type=MESH,
        )
        self.count += 1
        self.all.append(copy)
        copy.start()
        return copy

    def finish(self):
        for copy in self.all:
            copy.wait_send()


def rows16(index):
    return pl.ds(pl.multiple_of(index * PIECE, PIECE), PIECE)


def sub(index):
    return pl.ds(pl.multiple_of(index * WSUB, 16), WSUB)


COPIES = 192
HALVES = (slice(0, 512), slice(512, DE))
GROUP = 8
TILE = 256
ROWS = 2 * NLEN


def dot(a, b):
    return jnp.dot(a, b, preferred_element_type=F32)


def dot_nt(a, b):
    return lax.dot_general(a, b, (((1,), (1,)), ((), ())), preferred_element_type=F32)


def dot_tn(a, b):
    return lax.dot_general(a, b, (((0,), (0,)), ((), ())), preferred_element_type=F32)


def encode(rows_ref, gain_ref, up, down, slope, inv):
    rows = rows_ref[...].reshape(ROWS, DE).astype(F32)
    inverse = lax.rsqrt(jnp.mean(rows * rows, axis=-1, keepdims=True) + EPS)
    inv[...] = inverse
    normed = (rows * inverse * gain_ref[...].reshape(1, DE)).astype(BF16)
    root = math.sqrt(2.0 / math.pi)
    before = dot(normed, up[...])
    square = before * before
    th = jnp.tanh(root * before * (1.0 + 0.044715 * square))
    half = 0.5 * (1.0 + th)
    slope[...] = half + 0.5 * before * (1.0 - th * th) * root * (1.0 + 3.0 * 0.044715 * square)
    return (rows + dot((before * half).astype(BF16), down[...])).astype(BF16)


def encode_back(encoded_grad, rows_ref, gain_ref, up, down, slope, inv):
    before_grad = (dot_nt(encoded_grad, down[...]) * slope[...]).astype(BF16)
    normed_grad = dot_nt(before_grad, up[...])
    rows = rows_ref[...].reshape(ROWS, DE).astype(F32)
    inverse = inv[...]
    scaled = gain_ref[...].reshape(1, DE) * normed_grad
    result = (
        encoded_grad.astype(F32)
        + inverse * scaled
        - rows
        * (inverse * inverse * inverse)
        * jnp.mean(rows * scaled, axis=-1, keepdims=True)
    )
    return result.astype(BF16)


def attention(first, count, q_all, g_all, kv, kvg, att, qg):
    zero = jnp.zeros((STRETCH, HD), BF16)
    units = [(h, i) for h in range(first, first + count) for i in range(2)]
    pairs, products, mixes = [], [], []
    for h, i in units:
        column, tokens = slice(h * HD, (h + 1) * HD), slice(i * STRETCH, (i + 1) * STRETCH)
        pair = jnp.concatenate(
            [
                jnp.concatenate([q_all[tokens, column], zero], axis=1),
                jnp.concatenate([zero, g_all[tokens, column]], axis=1),
            ],
            axis=0,
        )
        pairs.append(pair)
        products.append(dot_nt(pair, kv[h // 2, h % 2, i * NLEN : (i + 1) * NLEN, :]))
    for product in products:
        exponent = jnp.exp(product[:STRETCH] * SCALE)
        weights = exponent / jnp.sum(exponent, axis=-1, keepdims=True)
        prob_grad = product[STRETCH:]
        mean = jnp.sum(weights * prob_grad, axis=-1, keepdims=True)
        score_grad = weights * (prob_grad - mean) * SCALE
        mixes.append(jnp.concatenate([score_grad, weights], axis=0).astype(BF16))
    for (h, i), pair, mix in zip(units, pairs, mixes):
        column, tokens = slice(h * HD, (h + 1) * HD), slice(i * STRETCH, (i + 1) * STRETCH)
        keys = slice(i * NLEN, (i + 1) * NLEN)
        o = dot(mix, kv[h // 2, h % 2, keys, :])
        qg[tokens, column] = o[:STRETCH, :HD].astype(BF16)
        att[tokens, column] = o[STRETCH:, HD:].astype(BF16)
        kvg[h // 2, h % 2, keys, :] = dot_tn(mix, pair).astype(BF16)


def whole_kernel(
    slot_ref, gain_ref, pool_ref, wk_ref, wv_ref, up_ref, down_ref, q_ref, g_ref,
    att_ref, qg_ref, pg_ref, fin_ref,
    user, mid_a, mid_b, out_a, out_b, rows, wall, up, down, q_all, g_all, att, qg, slope, inv, enc, enc_other,
    enct, kv, kvg, kvg_other, part, pg,
    mid2_a, mid2_b, out2_a, out2_b, ya1, ya2, xa1, xa2, xb1, xb2, yb1, yb2,
    zbuf, fin, ssem, rsem, lsem,
):
    p = Place()
    z, c, x, y = p.z, p.c, p.x, p.y
    cp = Copies(ssem, rsem)

    def local(src, dst, index):
        return pltpu.make_async_copy(src, dst, lsem.at[index])

    def own_chunk(source):
        return local(source.at[x % 2, sub(y), :], wall.at[z, c, x, sub(y), :], 0)

    @pl.when(x < 2)
    def key_chunk():
        own_chunk(wk_ref).start()

    @pl.when(x >= 2)
    def value_chunk():
        own_chunk(wv_ref).start()

    own_slots = pl.ds(p.seq * CAP, CAP)
    mid, out = (mid_a, mid_b), (out_a, out_b)
    mid2, out2 = (mid2_a, mid2_b), (out2_a, out2_b)
    own_pool = [
        local(pool_ref.at[:, rows16(z), part_of], mid[n].at[own_slots], (1, 11)[n])
        for n, part_of in enumerate(HALVES)
    ]
    for copy in own_pool:
        copy.start()
    loads = [
        local(src, dst, 2 + n)
        for n, (src, dst) in enumerate(
            ((up_ref, up), (down_ref, down), (q_ref, q_all), (g_ref, g_all))
        )
    ]
    for load in loads:
        load.start()
    greet(
        [p.at_z(d) for d in range(1, NZ)] + [p.sibling()] + [p.at_dp(d) for d in range(1, NX * NX)]
    )

    own_chunk(wk_ref).wait()
    order = (4, 3, 5, 2, 6, 1, 7)

    def chunk(zz, xx, yy):
        return wall.at[zz, c, xx, sub(yy), :]

    wz = [cp.start(chunk(z, x, y), chunk(z, x, y), p.at_z(d)) for d in order]
    hop1, forward = [], []
    for n, part_of in enumerate(HALVES):
        hop1.append(
            {
                d: cp.start(
                    pool_ref.at[:, rows16(p.zs(d)), part_of], mid[n].at[own_slots], p.at_z(d)
                )
                for d in order
            }
        )
        forward.append(
            [cp.start(pool_ref.at[:, rows16(z), part_of], mid[n].at[own_slots], p.sibling())]
        )

    for copy in wz:
        copy.wait_recv()
    lo, hi = pl.ds(0, 4), pl.ds(4, 4)

    def ring(region, heads, places, at):
        src = region(heads, places(0))
        return [cp.start(src, src, at(1)), cp.start(src, src, at(-1))]

    def ring2(region, first, places, at, arrived):
        arrived[0].wait_recv()
        src = region(pl.ds(first, 2), places(-1))
        one = cp.start(src, src, at(1))
        arrived[1].wait_recv()
        src = region(pl.ds(first + 2, 2), places(1))
        return [one, cp.start(src, src, at(-1))]

    def row_x(heads, xx):
        return wall.at[heads, c, xx, sub(y), :]

    def row_y(heads, yy):
        return wall.at[heads, c, x, sub(yy), :]

    def wide_y(heads, yy):
        return wall.at[heads, c, :, sub(yy), :]

    def wide_x(heads, xx):
        return wall.at[heads, c, xx, :, :]

    sib = []

    def share(src):
        sib.append(cp.start(src, src, p.sibling()))

    hop2 = []
    own_rows = [
        local(out[n].at[0], rows.at[:, rows16(z), part_of], (6, 12)[n])
        for n, part_of in enumerate(HALVES)
    ]

    def pool_step(n):
        for d in (1, 7, 2, 6, 3, 5, 4):
            hop1[n][d].wait_recv()
            block = mid[n].at[pl.ds((p.zs(-d) * 2 + c) * CAP, CAP)]
            forward[n].append(cp.start(block, block, p.sibling()))
        own_pool[n].wait()
        for copy in forward[n]:
            copy.wait_recv()
        for d in order + (0,):
            target = p.zs(d) * 2 + c
            for i in range(2):
                out[n][d, i] = mid[n][slot_ref[target * 2 + i]]
            if d == 0:
                own_rows[n].start()
            else:
                dst = rows.at[:, rows16(z), HALVES[n]]
                hop2.append(cp.start(out[n].at[d], dst, p.at_z(d)))

    a1 = ring(row_x, lo, p.xs, p.at_x)
    b1 = ring(row_y, hi, p.ys, p.at_y)
    a2 = ring2(row_x, 0, p.xs, p.at_x, a1)
    b2 = ring2(row_y, 4, p.ys, p.at_y, b1)
    for copy in a2:
        copy.wait_recv()
    a3 = ring(wide_y, lo, p.ys, p.at_y)
    for copy in b2:
        copy.wait_recv()
    b3 = ring(wide_x, hi, p.xs, p.at_x)
    share(wide_y(lo, y))
    share(wide_x(hi, x))
    def find_user(k, carry):
        slot = (p.zs(k // CAP) * 2 + c) * CAP + k % CAP
        found = jnp.int32(0)
        for stretch in range(SLOTS // 2):
            found = jnp.where(slot_ref[stretch] == slot, stretch + 1, found)
        user[k] = found
        return carry

    lax.fori_loop(0, NZ * CAP, find_user, 0)
    pool_step(0)
    a4 = ring2(wide_y, 0, p.ys, p.at_y, a3)
    b4 = ring2(wide_x, 4, p.xs, p.at_x, b3)
    for d in (1, -1):
        share(wide_y(lo, p.ys(d)))
        share(wide_x(hi, p.xs(d)))
    pool_step(1)
    for side in range(2):
        a4[side].wait_recv()
        share(wide_y(pl.ds(2 * side, 2), p.ys(2)))
        b4[side].wait_recv()
        share(wide_x(pl.ds(4 + 2 * side, 2), p.xs(2)))
    for copy in own_rows:
        copy.wait()
    for copy in hop2:
        copy.wait_recv()

    for load in loads:
        load.wait()
    encoded = encode(rows, gain_ref, up, down, slope, inv)
    enc[...] = encoded
    enc_sent = cp.start(enc, enc_other, p.sibling())
    enct[:, :ROWS] = encoded.T
    for copy in sib:
        copy.wait_recv()

    def both(h):
        k = wall[h // 2, h % 2, pl.ds(0, 2)].reshape(DE, HD)
        v = wall[h // 2, h % 2, pl.ds(2, 2)].reshape(DE, HD)
        return jnp.concatenate([k, v], axis=1)

    kvg_sent = []
    for first in range(0, HEADS, GROUP):
        for h in range(first, first + GROUP):
            kv[h // 2, h % 2] = dot(enc[...], both(h)).astype(BF16)
        attention(first, GROUP, q_all, g_all, kv, kvg, att, qg)
        span = pl.ds(first // 2, GROUP // 2)
        kvg_sent.append(cp.start(kvg.at[span, 1 - c], kvg_other.at[span], p.sibling()))
    results = [local(att, att_ref, 7), local(qg, qg_ref, 8)]
    for result in results:
        result.start()
    enc_sent.wait_recv()
    enct[:, ROWS:] = enc_other[...].T

    def weight_grad(h):
        grads = jnp.concatenate([kvg[h, c], kvg_other[h]], axis=0)
        block = dot(enct[...], grads).astype(BF16)
        for n in range(4):
            part[h, n] = block[(n % 2) * WROWS : (n % 2 + 1) * WROWS, (n // 2) * HD : (n // 2 + 1) * HD]

    def sum_y(first, count, yy):
        return part.at[pl.ds(first, count), :, sub(yy), :]

    def sum_x(first, count, xx):
        return part.at[pl.ds(first, count), xx, :, :]

    def narrow_x(first, count, xx):
        return part.at[pl.ds(first, count), xx, sub(y), :]

    def narrow_y(first, count, yy):
        return part.at[pl.ds(first, count), x, sub(yy), :]

    def far(region, first, places, at, land):
        return [
            cp.start(region(first, 2, places(2)), land.at[0], at(1)),
            cp.start(region(first + 2, 2, places(2)), land.at[1], at(-1)),
        ]

    def near(region, first, places, at, arrived, land1, land2):
        sent = []
        for side, d in ((0, 1), (1, -1)):
            arrived[side].wait_recv()
            block = region(first + 2 * side, 2, places(d))
            block[...] = (block[...].astype(F32) + land1[side].astype(F32)).astype(BF16)
            sent.append(cp.start(region(first, 4, places(d)), land2.at[side], at(d)))
        return sent

    def close(region, first, places, arrived, land2):
        for copy in arrived:
            copy.wait_recv()
        block = region(first, 4, places(0))
        block[...] = (
            block[...].astype(F32) + land2[0].astype(F32) + land2[1].astype(F32)
        ).astype(BF16)

    kvg_sent[0].wait_recv()
    for h in range(4):
        weight_grad(h)
    a1 = far(sum_y, 0, p.ys, p.at_y, ya1)
    kvg_sent[1].wait_recv()
    for h in range(4, NZ):
        weight_grad(h)
    b1 = far(sum_x, 4, p.xs, p.at_x, xb1)

    total = jnp.zeros((ROWS, DE), F32)
    for h in range(HEADS):
        total = total + dot_nt(kvg[h // 2, h % 2], both(h))
    pg[...] = encode_back(
        total.astype(BF16), rows, gain_ref, up, down, slope, inv
    ).reshape(2, NLEN, DE)

    own_two = pl.ds(p.seq * 2 + 1, 2)
    own_mid, back1, returns, back2, own_back = [], [], [], [], []
    for n, part_of in enumerate(HALVES):
        own_mid.append(local(pg.at[:, rows16(z), part_of], mid2[n].at[own_two], (9, 13)[n]))
        own_mid[n].start()
        back1.append(
            {
                d: cp.start(pg.at[:, rows16(p.zs(d)), part_of], mid2[n].at[own_two], p.at_z(d))
                for d in order
            }
        )
        returns.append(
            [cp.start(pg.at[:, rows16(z), part_of], mid2[n].at[own_two], p.sibling())]
        )
        mid2[n][0] = jnp.zeros(mid2[n].shape[1:], BF16)
        own_back.append(local(out2[n].at[0], pg_ref.at[:, rows16(z), part_of], (10, 14)[n]))

    def back_step(n):
        for d in (1, 7, 2, 6, 3, 5, 4):
            back1[n][d].wait_recv()
            block = mid2[n].at[pl.ds((p.zs(-d) * 2 + c) * 2 + 1, 2)]
            returns[n].append(cp.start(block, block, p.sibling()))
        own_mid[n].wait()
        for copy in returns[n]:
            copy.wait_recv()
        for d in order + (0,):
            for j in range(CAP):
                out2[n][d, j] = mid2[n][user[d * CAP + j]]
            if d == 0:
                own_back[n].start()
            else:
                dst = pg_ref.at[:, rows16(z), HALVES[n]]
                back2.append(cp.start(out2[n].at[d], dst, p.at_z(d)))

    a2 = near(sum_y, 0, p.ys, p.at_y, a1, ya1, ya2)
    b2 = near(sum_x, 4, p.xs, p.at_x, b1, xb1, xb2)
    back_step(0)
    back_step(1)
    close(sum_y, 0, p.ys, a2, ya2)
    a3 = far(narrow_x, 0, p.xs, p.at_x, xa1)
    close(sum_x, 4, p.xs, b2, xb2)
    b3 = far(narrow_y, 4, p.ys, p.at_y, yb1)
    a4 = near(narrow_x, 0, p.xs, p.at_x, a3, xa1, xa2)
    b4 = near(narrow_y, 4, p.ys, p.at_y, b3, yb1, yb2)
    close(narrow_x, 0, p.xs, a4, xa2)
    close(narrow_y, 4, p.ys, b4, yb2)
    zsum = [cp.start(part.at[p.zs(d), x, sub(y), :], zbuf.at[d], p.at_z(d)) for d in order]
    for copy in zsum:
        copy.wait_recv()
    total = part[z, x, sub(y), :].astype(F32)
    for d in range(1, NZ):
        total = total + zbuf[d].astype(F32)
    fin[x, y] = total.astype(BF16)
    last = [cp.start(fin.at[x, y], fin.at[x, y], p.at_dp(d)) for d in range(1, NX * NX)]
    for copy in last:
        copy.wait_recv()
    written = local(fin, fin_ref, 15)
    written.start()
    for copy in own_back:
        copy.wait()
    for result in results:
        result.wait()
    for copy in back2:
        copy.wait_recv()
    written.wait()
    cp.finish()


def whole(slots, gain, pool, wk, wv, up, down, queries, grads):
    anyspace = pl.BlockSpec(memory_space=pl.ANY)
    vmem = pl.BlockSpec(memory_space=pltpu.VMEM)
    width = HEADS * HD

    def scratch(*shape):
        return pltpu.VMEM(shape, BF16)

    return pl.pallas_call(
        whole_kernel,
        out_shape=(
            jax.ShapeDtypeStruct((TOKENS, width), BF16),
            jax.ShapeDtypeStruct((TOKENS, width), BF16),
            jax.ShapeDtypeStruct((CAP, NLEN, DE), BF16),
            jax.ShapeDtypeStruct((NX, NX, WSUB, HD), BF16),
        ),
        in_specs=[pl.BlockSpec(memory_space=pltpu.SMEM), vmem] + [anyspace] * 7,
        out_specs=(anyspace,) * 4,
        scratch_shapes=[
            pltpu.SMEM((NZ * CAP,), jnp.int32),
            scratch(SLOTS, PIECE, 512),
            scratch(SLOTS, PIECE, DE - 512),
            scratch(NZ, 2, PIECE, 512),
            scratch(NZ, 2, PIECE, DE - 512),
            scratch(2, NLEN, DE),
            scratch(NZ, 2, 4, WROWS, HD),
            scratch(DE, FFE),
            scratch(FFE, DE),
            scratch(TOKENS, width),
            scratch(TOKENS, width),
            scratch(TOKENS, width),
            scratch(TOKENS, width),
            pltpu.VMEM((ROWS, FFE), F32),
            pltpu.VMEM((ROWS, 1), F32),
            scratch(ROWS, DE),
            scratch(ROWS, DE),
            scratch(DE, 2 * ROWS),
            scratch(NZ, 2, ROWS, 2 * HD),
            scratch(NZ, 2, ROWS, 2 * HD),
            scratch(NZ, ROWS, 2 * HD),
            scratch(NZ, 4, WROWS, HD),
            scratch(2, NLEN, DE),
            scratch(1 + SLOTS // 2, PIECE, 512),
            scratch(1 + SLOTS // 2, PIECE, DE - 512),
            scratch(NZ, CAP, PIECE, 512),
            scratch(NZ, CAP, PIECE, DE - 512),
            scratch(2, 2, 4, WSUB, HD),
            scratch(2, 4, 4, WSUB, HD),
            scratch(2, 2, WSUB, HD),
            scratch(2, 4, WSUB, HD),
            scratch(2, 2, WROWS, HD),
            scratch(2, 4, WROWS, HD),
            scratch(2, 2, WSUB, HD),
            scratch(2, 4, WSUB, HD),
            scratch(NZ, WSUB, HD),
            scratch(NX, NX, WSUB, HD),
            pltpu.SemaphoreType.DMA((COPIES,)),
            pltpu.SemaphoreType.DMA((COPIES,)),
            pltpu.SemaphoreType.DMA((16,)),
        ],
        compiler_params=pltpu.CompilerParams(
            collective_id=0, has_side_effects=True, vmem_limit_bytes=56 * 1024 * 1024
        ),
        name="whole",
    )(slots, gain, pool, wk, wv, up, down, queries, grads)


def place_kernel(att, qg, pg, fin, att_out, qg_out, pg_out, kw_out, vw_out, wide, key, value, sems):
    load = pltpu.make_async_copy(fin, wide, sems.at[0])
    load.start()
    copies = []
    for src, dst, cut in ((pg, pg_out, 4), (att, att_out, 2), (qg, qg_out, 2)):
        size = src.shape[0] // cut
        for n in range(cut):
            span = pl.ds(n * size, size)
            copies.append(
                pltpu.make_async_copy(src.at[span], dst.at[span], sems.at[1 + len(copies)])
            )
            copies[-1].start()
    load.wait()
    for n, (held, dst) in enumerate(((key, kw_out), (value, vw_out))):
        held[...] = wide[2 * n : 2 * n + 2].reshape(DE, HD).astype(F32)
        copies.append(pltpu.make_async_copy(held, dst, sems.at[1 + len(copies)]))
        copies[-1].start()
    for copy in copies:
        copy.wait()


def place(att, qg, pg, fin):
    anyspace = pl.BlockSpec(memory_space=pl.ANY)
    shapes = [jax.ShapeDtypeStruct(a.shape, a.dtype) for a in (att, qg, pg)]
    grad = jax.ShapeDtypeStruct((DE, HD), F32)
    return pl.pallas_call(
        place_kernel,
        out_shape=(*shapes, grad, grad),
        in_specs=[anyspace] * 4,
        out_specs=(anyspace,) * 5,
        scratch_shapes=[
            pltpu.VMEM((NX, NX, WSUB, HD), BF16),
            pltpu.VMEM((DE, HD), F32),
            pltpu.VMEM((DE, HD), F32),
            pltpu.SemaphoreType.DMA((11,)),
        ],
        compiler_params=pltpu.CompilerParams(vmem_limit_bytes=56 * 1024 * 1024),
        name="place",
    )(att, qg, pg, fin)


def on_device(queries, attended_grad, pool, stretch_slot, gain, up, down, key_w, value_w):
    attended, query_grad, pool_grad, key_grad, value_grad = place(
        *whole(
            stretch_slot[0],
            gain,
            pool[0],
            key_w.reshape(2, WROWS, HD),
            value_w.reshape(2, WROWS, HD),
            up,
            down,
            queries[0],
            attended_grad[0],
        )
    )
    return attended[None], query_grad[None], pool_grad[None], key_grad, value_grad


def solution(mesh):
    return jax.shard_map(
        on_device,
        mesh=mesh,
        in_specs=(
            P("dp", "seq", None),
            P("dp", "seq", None),
            P("dp", "seq", None, None),
            P("dp", None),
            P(),
            P(),
            P(),
            P(None, "seq"),
            P(None, "seq"),
        ),
        out_specs=(
            P("dp", "seq", None),
            P("dp", "seq", None),
            P("dp", "seq", None, None),
            P(None, "seq"),
            P(None, "seq"),
        ),
        check_vma=False,
    )
```

```python
import math

import jax
import jax.numpy as jnp
from jax import lax
from jax.experimental import pallas as pl
from jax.experimental.pallas import tpu as pltpu
from jax.sharding import PartitionSpec as P

STRETCH = 64
HD = 128
NX = 4
NZ = 8
CAP = 4
SLOTS = 64
NLEN = 128
PIECE = 16
DE = 896
FFE = 1792
HEADS = 16
WROWS = 448
WSUB = 112
TOKENS = 128
EPS = 1e-6
SCALE = 1.0 / math.sqrt(HD)

MESH = pl.DeviceIdType.MESH
BF16 = jnp.bfloat16
F32 = jnp.float32


class Place:
    def __init__(self):
        self.dp = lax.axis_index("dp")
        self.seq = lax.axis_index("seq")
        self.x = self.dp // NX
        self.y = self.dp % NX
        self.z = self.seq // 2
        self.c = self.seq % 2

    def xs(self, d):
        return (self.x + d + NX) % NX

    def ys(self, d):
        return (self.y + d + NX) % NX

    def zs(self, d):
        return (self.z + d + NZ) % NZ

    def at_x(self, d):
        return (self.xs(d) * NX + self.y, self.seq)

    def at_y(self, d):
        return (self.x * NX + self.ys(d), self.seq)

    def at_z(self, d):
        return (self.dp, self.zs(d) * 2 + self.c)

    def at_dp(self, d):
        return ((self.dp + d) % (NX * NX), self.seq)

    def sibling(self):
        return (self.dp, self.z * 2 + 1 - self.c)


def greet(partners):
    barrier = pltpu.get_barrier_semaphore()
    for partner in partners:
        pl.semaphore_signal(barrier, inc=1, device_id=partner, device_id_type=MESH)
    pl.semaphore_wait(barrier, len(partners))


class Copies:
    def __init__(self, send_sems, recv_sems):
        self.send_sems, self.recv_sems = send_sems, recv_sems
        self.count = 0
        self.all = []

    def start(self, src, dst, device):
        copy = pltpu.make_async_remote_copy(
            src_ref=src,
            dst_ref=dst,
            send_sem=self.send_sems.at[self.count],
            recv_sem=self.recv_sems.at[self.count],
            device_id=device,
            device_id_type=MESH,
        )
        self.count += 1
        self.all.append(copy)
        copy.start()
        return copy

    def finish(self):
        for copy in self.all:
            copy.wait_send()


def rows16(index):
    return pl.ds(pl.multiple_of(index * PIECE, PIECE), PIECE)


def sub(index):
    return pl.ds(pl.multiple_of(index * WSUB, 16), WSUB)


COPIES = 192
HALVES = (slice(0, 512), slice(512, DE))
GROUP = 8
TILE = 256
ROWS = 2 * NLEN


def dot(a, b):
    return jnp.dot(a, b, preferred_element_type=F32)


def dot_nt(a, b):
    return lax.dot_general(a, b, (((1,), (1,)), ((), ())), preferred_element_type=F32)


def dot_tn(a, b):
    return lax.dot_general(a, b, (((0,), (0,)), ((), ())), preferred_element_type=F32)


def encode(rows_ref, gain_ref, up, down, slope, inv):
    rows = rows_ref[...].reshape(ROWS, DE).astype(F32)
    inverse = lax.rsqrt(jnp.mean(rows * rows, axis=-1, keepdims=True) + EPS)
    inv[...] = inverse
    normed = (rows * inverse * gain_ref[...].reshape(1, DE)).astype(BF16)
    root = math.sqrt(2.0 / math.pi)
    before = dot(normed, up[...])
    square = before * before
    th = jnp.tanh(root * before * (1.0 + 0.044715 * square))
    half = 0.5 * (1.0 + th)
    slope[...] = half + 0.5 * before * (1.0 - th * th) * root * (1.0 + 3.0 * 0.044715 * square)
    return (rows + dot((before * half).astype(BF16), down[...])).astype(BF16)


def encode_back(encoded_grad, rows_ref, gain_ref, up, down, slope, inv):
    before_grad = (dot_nt(encoded_grad, down[...]) * slope[...]).astype(BF16)
    normed_grad = dot_nt(before_grad, up[...])
    rows = rows_ref[...].reshape(ROWS, DE).astype(F32)
    inverse = inv[...]
    scaled = gain_ref[...].reshape(1, DE) * normed_grad
    result = (
        encoded_grad.astype(F32)
        + inverse * scaled
        - rows
        * (inverse * inverse * inverse)
        * jnp.mean(rows * scaled, axis=-1, keepdims=True)
    )
    return result.astype(BF16)


def attention(first, count, q_all, g_all, kv, kvg, att, qg):
    zero = jnp.zeros((STRETCH, HD), BF16)
    units = [(h, i) for h in range(first, first + count) for i in range(2)]
    pairs, products, mixes = [], [], []
    for h, i in units:
        column, tokens = slice(h * HD, (h + 1) * HD), slice(i * STRETCH, (i + 1) * STRETCH)
        pair = jnp.concatenate(
            [
                jnp.concatenate([q_all[tokens, column], zero], axis=1),
                jnp.concatenate([zero, g_all[tokens, column]], axis=1),
            ],
            axis=0,
        )
        pairs.append(pair)
        products.append(dot_nt(pair, kv[h // 2, h % 2, i * NLEN : (i + 1) * NLEN, :]))
    for product in products:
        exponent = jnp.exp(product[:STRETCH] * SCALE)
        weights = exponent / jnp.sum(exponent, axis=-1, keepdims=True)
        prob_grad = product[STRETCH:]
        mean = jnp.sum(weights * prob_grad, axis=-1, keepdims=True)
        score_grad = weights * (prob_grad - mean) * SCALE
        mixes.append(jnp.concatenate([score_grad, weights], axis=0).astype(BF16))
    for (h, i), pair, mix in zip(units, pairs, mixes):
        column, tokens = slice(h * HD, (h + 1) * HD), slice(i * STRETCH, (i + 1) * STRETCH)
        keys = slice(i * NLEN, (i + 1) * NLEN)
        o = dot(mix, kv[h // 2, h % 2, keys, :])
        qg[tokens, column] = o[:STRETCH, :HD].astype(BF16)
        att[tokens, column] = o[STRETCH:, HD:].astype(BF16)
        kvg[h // 2, h % 2, keys, :] = dot_tn(mix, pair).astype(BF16)


def whole_kernel(
    slot_ref, gain_ref, pool_ref, wk_ref, wv_ref, up_ref, down_ref, q_ref, g_ref,
    att_ref, qg_ref, pg_ref, fin_ref,
    user, mid_a, mid_b, out_a, out_b, rows, wall, up, down, q_all, g_all, att, qg, slope, inv, enc, enc_other,
    enct, kv, kvg, kvg_other, part, pg,
    mid2_a, mid2_b, out2_a, out2_b, ya1, ya2, xa1, xa2, xb1, xb2, yb1, yb2,
    zbuf, fin, ssem, rsem, lsem,
):
    p = Place()
    z, c, x, y = p.z, p.c, p.x, p.y
    cp = Copies(ssem, rsem)

    def local(src, dst, index):
        return pltpu.make_async_copy(src, dst, lsem.at[index])

    def own_chunk(source):
        return local(source.at[x % 2, sub(y), :], wall.at[z, c, x, sub(y), :], 0)

    @pl.when(x < 2)
    def key_chunk():
        own_chunk(wk_ref).start()

    @pl.when(x >= 2)
    def value_chunk():
        own_chunk(wv_ref).start()

    own_slots = pl.ds(p.seq * CAP, CAP)
    mid, out = (mid_a, mid_b), (out_a, out_b)
    mid2, out2 = (mid2_a, mid2_b), (out2_a, out2_b)
    own_pool = [
        local(pool_ref.at[:, rows16(z), part_of], mid[n].at[own_slots], (1, 11)[n])
        for n, part_of in enumerate(HALVES)
    ]
    for copy in own_pool:
        copy.start()
    loads = [
        local(src, dst, 2 + n)
        for n, (src, dst) in enumerate(
            ((up_ref, up), (down_ref, down), (q_ref, q_all), (g_ref, g_all))
        )
    ]
    for load in loads:
        load.start()
    greet(
        [p.at_z(d) for d in range(1, NZ)] + [p.sibling()] + [p.at_dp(d) for d in range(1, NX * NX)]
    )

    own_chunk(wk_ref).wait()
    order = (4, 3, 5, 2, 6, 1, 7)

    def chunk(zz, xx, yy):
        return wall.at[zz, c, xx, sub(yy), :]

    wz = [cp.start(chunk(z, x, y), chunk(z, x, y), p.at_z(d)) for d in order]
    hop1, forward = [], []
    for n, part_of in enumerate(HALVES):
        hop1.append(
            {
                d: cp.start(
                    pool_ref.at[:, rows16(p.zs(d)), part_of], mid[n].at[own_slots], p.at_z(d)
                )
                for d in order
            }
        )
        forward.append(
            [cp.start(pool_ref.at[:, rows16(z), part_of], mid[n].at[own_slots], p.sibling())]
        )

    for copy in wz:
        copy.wait_recv()
    lo, hi = pl.ds(0, 4), pl.ds(4, 4)

    def ring(region, heads, places, at):
        src = region(heads, places(0))
        return [cp.start(src, src, at(1)), cp.start(src, src, at(-1))]

    def ring2(region, first, places, at, arrived):
        arrived[0].wait_recv()
        src = region(pl.ds(first, 2), places(-1))
        one = cp.start(src, src, at(1))
        arrived[1].wait_recv()
        src = region(pl.ds(first + 2, 2), places(1))
        return [one, cp.start(src, src, at(-1))]

    def row_x(heads, xx):
        return wall.at[heads, c, xx, sub(y), :]

    def row_y(heads, yy):
        return wall.at[heads, c, x, sub(yy), :]

    def wide_y(heads, yy):
        return wall.at[heads, c, :, sub(yy), :]

    def wide_x(heads, xx):
        return wall.at[heads, c, xx, :, :]

    sib = []

    def share(src):
        sib.append(cp.start(src, src, p.sibling()))

    hop2 = []
    own_rows = [
        local(out[n].at[0], rows.at[:, rows16(z), part_of], (6, 12)[n])
        for n, part_of in enumerate(HALVES)
    ]

    def pool_step(n):
        for d in (1, 7, 2, 6, 3, 5, 4):
            hop1[n][d].wait_recv()
            block = mid[n].at[pl.ds((p.zs(-d) * 2 + c) * CAP, CAP)]
            forward[n].append(cp.start(block, block, p.sibling()))
        own_pool[n].wait()
        for copy in forward[n]:
            copy.wait_recv()
        for d in order + (0,):
            target = p.zs(d) * 2 + c
            for i in range(2):
                out[n][d, i] = mid[n][slot_ref[target * 2 + i]]
            if d == 0:
                own_rows[n].start()
            else:
                dst = rows.at[:, rows16(z), HALVES[n]]
                hop2.append(cp.start(out[n].at[d], dst, p.at_z(d)))

    a1 = ring(row_x, lo, p.xs, p.at_x)
    b1 = ring(row_y, hi, p.ys, p.at_y)
    a2 = ring2(row_x, 0, p.xs, p.at_x, a1)
    b2 = ring2(row_y, 4, p.ys, p.at_y, b1)
    for copy in a2:
        copy.wait_recv()
    a3 = ring(wide_y, lo, p.ys, p.at_y)
    for copy in b2:
        copy.wait_recv()
    b3 = ring(wide_x, hi, p.xs, p.at_x)
    share(wide_y(lo, y))
    share(wide_x(hi, x))
    def find_user(k, carry):
        slot = (p.zs(k // CAP) * 2 + c) * CAP + k % CAP
        found = jnp.int32(0)
        for stretch in range(SLOTS // 2):
            found = jnp.where(slot_ref[stretch] == slot, stretch + 1, found)
        user[k] = found
        return carry

    lax.fori_loop(0, NZ * CAP, find_user, 0)
    pool_step(0)
    a4 = ring2(wide_y, 0, p.ys, p.at_y, a3)
    b4 = ring2(wide_x, 4, p.xs, p.at_x, b3)
    for d in (1, -1):
        share(wide_y(lo, p.ys(d)))
        share(wide_x(hi, p.xs(d)))
    for side in range(2):
        a4[side].wait_recv()
        share(wide_y(pl.ds(2 * side, 2), p.ys(2)))
        b4[side].wait_recv()
        share(wide_x(pl.ds(4 + 2 * side, 2), p.xs(2)))
    pool_step(1)
    for copy in own_rows:
        copy.wait()
    for copy in hop2:
        copy.wait_recv()

    for load in loads:
        load.wait()
    encoded = encode(rows, gain_ref, up, down, slope, inv)
    enc[...] = encoded
    enc_sent = cp.start(enc, enc_other, p.sibling())
    enct[:, :ROWS] = encoded.T
    for copy in sib:
        copy.wait_recv()

    def both(h):
        k = wall[h // 2, h % 2, pl.ds(0, 2)].reshape(DE, HD)
        v = wall[h // 2, h % 2, pl.ds(2, 2)].reshape(DE, HD)
        return jnp.concatenate([k, v], axis=1)

    kvg_sent = []
    for first in range(0, HEADS, GROUP):
        for h in range(first, first + GROUP):
            kv[h // 2, h % 2] = dot(enc[...], both(h)).astype(BF16)
        attention(first, GROUP, q_all, g_all, kv, kvg, att, qg)
        span = pl.ds(first // 2, GROUP // 2)
        kvg_sent.append(cp.start(kvg.at[span, 1 - c], kvg_other.at[span], p.sibling()))
    results = [local(att, att_ref, 7), local(qg, qg_ref, 8)]
    for result in results:
        result.start()
    enc_sent.wait_recv()
    enct[:, ROWS:] = enc_other[...].T

    def weight_grad(h):
        grads = jnp.concatenate([kvg[h, c], kvg_other[h]], axis=0)
        block = dot(enct[...], grads).astype(BF16)
        for n in range(4):
            part[h, n] = block[(n % 2) * WROWS : (n % 2 + 1) * WROWS, (n // 2) * HD : (n // 2 + 1) * HD]

    def sum_y(first, count, yy):
        return part.at[pl.ds(first, count), :, sub(yy), :]

    def sum_x(first, count, xx):
        return part.at[pl.ds(first, count), xx, :, :]

    def narrow_x(first, count, xx):
        return part.at[pl.ds(first, count), xx, sub(y), :]

    def narrow_y(first, count, yy):
        return part.at[pl.ds(first, count), x, sub(yy), :]

    def far(region, first, places, at, land):
        return [
            cp.start(region(first, 2, places(2)), land.at[0], at(1)),
            cp.start(region(first + 2, 2, places(2)), land.at[1], at(-1)),
        ]

    def near(region, first, places, at, arrived, land1, land2):
        sent = []
        for side, d in ((0, 1), (1, -1)):
            arrived[side].wait_recv()
            block = region(first + 2 * side, 2, places(d))
            block[...] = (block[...].astype(F32) + land1[side].astype(F32)).astype(BF16)
            sent.append(cp.start(region(first, 4, places(d)), land2.at[side], at(d)))
        return sent

    def close(region, first, places, arrived, land2):
        for copy in arrived:
            copy.wait_recv()
        block = region(first, 4, places(0))
        block[...] = (
            block[...].astype(F32) + land2[0].astype(F32) + land2[1].astype(F32)
        ).astype(BF16)

    kvg_sent[0].wait_recv()
    for h in range(4):
        weight_grad(h)
    a1 = far(sum_y, 0, p.ys, p.at_y, ya1)
    kvg_sent[1].wait_recv()
    for h in range(4, NZ):
        weight_grad(h)
    b1 = far(sum_x, 4, p.xs, p.at_x, xb1)

    total = jnp.zeros((ROWS, DE), F32)
    for h in range(HEADS):
        total = total + dot_nt(kvg[h // 2, h % 2], both(h))
    pg[...] = encode_back(
        total.astype(BF16), rows, gain_ref, up, down, slope, inv
    ).reshape(2, NLEN, DE)

    own_two = pl.ds(p.seq * 2 + 1, 2)
    own_mid, back1, returns, back2, own_back = [], [], [], [], []
    for n, part_of in enumerate(HALVES):
        own_mid.append(local(pg.at[:, rows16(z), part_of], mid2[n].at[own_two], (9, 13)[n]))
        own_mid[n].start()
        back1.append(
            {
                d: cp.start(pg.at[:, rows16(p.zs(d)), part_of], mid2[n].at[own_two], p.at_z(d))
                for d in order
            }
        )
        returns.append(
            [cp.start(pg.at[:, rows16(z), part_of], mid2[n].at[own_two], p.sibling())]
        )
        mid2[n][0] = jnp.zeros(mid2[n].shape[1:], BF16)
        own_back.append(local(out2[n].at[0], pg_ref.at[:, rows16(z), part_of], (10, 14)[n]))

    def back_step(n):
        for d in (1, 7, 2, 6, 3, 5, 4):
            back1[n][d].wait_recv()
            block = mid2[n].at[pl.ds((p.zs(-d) * 2 + c) * 2 + 1, 2)]
            returns[n].append(cp.start(block, block, p.sibling()))
        own_mid[n].wait()
        for copy in returns[n]:
            copy.wait_recv()
        for d in order + (0,):
            for j in range(CAP):
                out2[n][d, j] = mid2[n][user[d * CAP + j]]

    def back_send(n):
        for d in order + (0,):
            if d == 0:
                own_back[n].start()
            else:
                dst = pg_ref.at[:, rows16(z), HALVES[n]]
                back2.append(cp.start(out2[n].at[d], dst, p.at_z(d)))

    a2 = near(sum_y, 0, p.ys, p.at_y, a1, ya1, ya2)
    b2 = near(sum_x, 4, p.xs, p.at_x, b1, xb1, xb2)
    back_step(0)
    back_send(0)
    back_step(1)
    close(sum_y, 0, p.ys, a2, ya2)
    a3 = far(narrow_x, 0, p.xs, p.at_x, xa1)
    close(sum_x, 4, p.xs, b2, xb2)
    b3 = far(narrow_y, 4, p.ys, p.at_y, yb1)
    a4 = near(narrow_x, 0, p.xs, p.at_x, a3, xa1, xa2)
    b4 = near(narrow_y, 4, p.ys, p.at_y, b3, yb1, yb2)
    close(narrow_x, 0, p.xs, a4, xa2)
    close(narrow_y, 4, p.ys, b4, yb2)
    zsum = [cp.start(part.at[p.zs(d), x, sub(y), :], zbuf.at[d], p.at_z(d)) for d in order]
    back_send(1)
    for copy in zsum:
        copy.wait_recv()
    total = part[z, x, sub(y), :].astype(F32)
    for d in range(1, NZ):
        total = total + zbuf[d].astype(F32)
    fin[x, y] = total.astype(BF16)
    last = [cp.start(fin.at[x, y], fin.at[x, y], p.at_dp(d)) for d in range(1, NX * NX)]
    for copy in last:
        copy.wait_recv()
    written = local(fin, fin_ref, 15)
    written.start()
    for copy in own_back:
        copy.wait()
    for result in results:
        result.wait()
    for copy in back2:
        copy.wait_recv()
    written.wait()
    cp.finish()


def whole(slots, gain, pool, wk, wv, up, down, queries, grads):
    anyspace = pl.BlockSpec(memory_space=pl.ANY)
    vmem = pl.BlockSpec(memory_space=pltpu.VMEM)
    width = HEADS * HD

    def scratch(*shape):
        return pltpu.VMEM(shape, BF16)

    return pl.pallas_call(
        whole_kernel,
        out_shape=(
            jax.ShapeDtypeStruct((TOKENS, width), BF16),
            jax.ShapeDtypeStruct((TOKENS, width), BF16),
            jax.ShapeDtypeStruct((CAP, NLEN, DE), BF16),
            jax.ShapeDtypeStruct((NX, NX, WSUB, HD), BF16),
        ),
        in_specs=[pl.BlockSpec(memory_space=pltpu.SMEM), vmem] + [anyspace] * 7,
        out_specs=(anyspace,) * 4,
        scratch_shapes=[
            pltpu.SMEM((NZ * CAP,), jnp.int32),
            scratch(SLOTS, PIECE, 512),
            scratch(SLOTS, PIECE, DE - 512),
            scratch(NZ, 2, PIECE, 512),
            scratch(NZ, 2, PIECE, DE - 512),
            scratch(2, NLEN, DE),
            scratch(NZ, 2, 4, WROWS, HD),
            scratch(DE, FFE),
            scratch(FFE, DE),
            scratch(TOKENS, width),
            scratch(TOKENS, width),
            scratch(TOKENS, width),
            scratch(TOKENS, width),
            pltpu.VMEM((ROWS, FFE), F32),
            pltpu.VMEM((ROWS, 1), F32),
            scratch(ROWS, DE),
            scratch(ROWS, DE),
            scratch(DE, 2 * ROWS),
            scratch(NZ, 2, ROWS, 2 * HD),
            scratch(NZ, 2, ROWS, 2 * HD),
            scratch(NZ, ROWS, 2 * HD),
            scratch(NZ, 4, WROWS, HD),
            scratch(2, NLEN, DE),
            scratch(1 + SLOTS // 2, PIECE, 512),
            scratch(1 + SLOTS // 2, PIECE, DE - 512),
            scratch(NZ, CAP, PIECE, 512),
            scratch(NZ, CAP, PIECE, DE - 512),
            scratch(2, 2, 4, WSUB, HD),
            scratch(2, 4, 4, WSUB, HD),
            scratch(2, 2, WSUB, HD),
            scratch(2, 4, WSUB, HD),
            scratch(2, 2, WROWS, HD),
            scratch(2, 4, WROWS, HD),
            scratch(2, 2, WSUB, HD),
            scratch(2, 4, WSUB, HD),
            scratch(NZ, WSUB, HD),
            scratch(NX, NX, WSUB, HD),
            pltpu.SemaphoreType.DMA((COPIES,)),
            pltpu.SemaphoreType.DMA((COPIES,)),
            pltpu.SemaphoreType.DMA((16,)),
        ],
        compiler_params=pltpu.CompilerParams(
            collective_id=0, has_side_effects=True, vmem_limit_bytes=56 * 1024 * 1024
        ),
        name="whole",
    )(slots, gain, pool, wk, wv, up, down, queries, grads)


def place_kernel(
    att, qg, pg, fin, att_out, qg_out, pg_out, kw_out, vw_out,
    wide, key, value, att_held, qg_held, pg_held, sems,
):
    loads, stores = [], []

    def move(src, held, dst):
        loads.append(pltpu.make_async_copy(src, held, sems.at[len(loads)]))
        stores.append(pltpu.make_async_copy(held, dst, sems.at[16 + len(stores)]))
        loads[-1].start()

    wide_load = pltpu.make_async_copy(fin, wide, sems.at[15])
    wide_load.start()
    for src, held, dst, cut in (
        (pg, pg_held, pg_out, 4),
        (att, att_held, att_out, 2),
        (qg, qg_held, qg_out, 2),
    ):
        size = src.shape[0] // cut
        for n in range(cut):
            span = pl.ds(n * size, size)
            move(src.at[span], held.at[span], dst.at[span])
    wide_load.wait()
    for n, (held, dst) in enumerate(((key, kw_out), (value, vw_out))):
        held[...] = wide[2 * n : 2 * n + 2].reshape(DE, HD).astype(F32)
        stores.append(pltpu.make_async_copy(held, dst, sems.at[16 + len(stores)]))
        stores[-1].start()
    for load, store in zip(loads, stores):
        load.wait()
        store.start()
    for store in stores:
        store.wait()


def place(att, qg, pg, fin):
    anyspace = pl.BlockSpec(memory_space=pl.ANY)
    shapes = [jax.ShapeDtypeStruct(a.shape, a.dtype) for a in (att, qg, pg)]
    grad = jax.ShapeDtypeStruct((DE, HD), F32)
    return pl.pallas_call(
        place_kernel,
        out_shape=(*shapes, grad, grad),
        in_specs=[anyspace] * 4,
        out_specs=(anyspace,) * 5,
        scratch_shapes=[
            pltpu.VMEM((NX, NX, WSUB, HD), BF16),
            pltpu.VMEM((DE, HD), F32),
            pltpu.VMEM((DE, HD), F32),
            pltpu.VMEM(att.shape, BF16),
            pltpu.VMEM(qg.shape, BF16),
            pltpu.VMEM(pg.shape, BF16),
            pltpu.SemaphoreType.DMA((32,)),
        ],
        compiler_params=pltpu.CompilerParams(vmem_limit_bytes=56 * 1024 * 1024),
        name="place",
    )(att, qg, pg, fin)


def on_device(queries, attended_grad, pool, stretch_slot, gain, up, down, key_w, value_w):
    attended, query_grad, pool_grad, key_grad, value_grad = place(
        *whole(
            stretch_slot[0],
            gain,
            pool[0],
            key_w.reshape(2, WROWS, HD),
            value_w.reshape(2, WROWS, HD),
            up,
            down,
            queries[0],
            attended_grad[0],
        )
    )
    return attended[None], query_grad[None], pool_grad[None], key_grad, value_grad


def solution(mesh):
    return jax.shard_map(
        on_device,
        mesh=mesh,
        in_specs=(
            P("dp", "seq", None),
            P("dp", "seq", None),
            P("dp", "seq", None, None),
            P("dp", None),
            P(),
            P(),
            P(),
            P(None, "seq"),
            P(None, "seq"),
        ),
        out_specs=(
            P("dp", "seq", None),
            P("dp", "seq", None),
            P("dp", "seq", None, None),
            P(None, "seq"),
            P(None, "seq"),
        ),
        check_vma=False,
    )
```

```python
import math

import jax
import jax.numpy as jnp
from jax import lax
from jax.experimental import pallas as pl
from jax.experimental.pallas import tpu as pltpu
from jax.sharding import PartitionSpec as P

STRETCH = 64
HD = 128
NX = 4
NZ = 8
CAP = 4
SLOTS = 64
NLEN = 128
PIECE = 16
DE = 896
FFE = 1792
HEADS = 16
WROWS = 448
WSUB = 112
TOKENS = 128
EPS = 1e-6
SCALE = 1.0 / math.sqrt(HD)

MESH = pl.DeviceIdType.MESH
BF16 = jnp.bfloat16
F32 = jnp.float32


class Place:
    def __init__(self):
        self.dp = lax.axis_index("dp")
        self.seq = lax.axis_index("seq")
        self.x = self.dp // NX
        self.y = self.dp % NX
        self.z = self.seq // 2
        self.c = self.seq % 2

    def xs(self, d):
        return (self.x + d + NX) % NX

    def ys(self, d):
        return (self.y + d + NX) % NX

    def zs(self, d):
        return (self.z + d + NZ) % NZ

    def at_x(self, d):
        return (self.xs(d) * NX + self.y, self.seq)

    def at_y(self, d):
        return (self.x * NX + self.ys(d), self.seq)

    def at_z(self, d):
        return (self.dp, self.zs(d) * 2 + self.c)

    def at_dp(self, d):
        return ((self.dp + d) % (NX * NX), self.seq)

    def sibling(self):
        return (self.dp, self.z * 2 + 1 - self.c)


def greet(partners):
    barrier = pltpu.get_barrier_semaphore()
    for partner in partners:
        pl.semaphore_signal(barrier, inc=1, device_id=partner, device_id_type=MESH)
    pl.semaphore_wait(barrier, len(partners))


class Copies:
    def __init__(self, send_sems, recv_sems):
        self.send_sems, self.recv_sems = send_sems, recv_sems
        self.count = 0
        self.all = []

    def start(self, src, dst, device):
        copy = pltpu.make_async_remote_copy(
            src_ref=src,
            dst_ref=dst,
            send_sem=self.send_sems.at[self.count],
            recv_sem=self.recv_sems.at[self.count],
            device_id=device,
            device_id_type=MESH,
        )
        self.count += 1
        self.all.append(copy)
        copy.start()
        return copy

    def finish(self):
        for copy in self.all:
            copy.wait_send()


def rows16(index):
    return pl.ds(pl.multiple_of(index * PIECE, PIECE), PIECE)


def sub(index):
    return pl.ds(pl.multiple_of(index * WSUB, 16), WSUB)


COPIES = 192
SPLIT = 640
HALVES = (slice(0, SPLIT), slice(SPLIT, DE))
GROUP = 8
TILE = 256
ROWS = 2 * NLEN


def dot(a, b):
    return jnp.dot(a, b, preferred_element_type=F32)


def dot_nt(a, b):
    return lax.dot_general(a, b, (((1,), (1,)), ((), ())), preferred_element_type=F32)


def dot_tn(a, b):
    return lax.dot_general(a, b, (((0,), (0,)), ((), ())), preferred_element_type=F32)


def encode(rows_ref, gain_ref, up, down, slope, inv):
    rows = rows_ref[...].reshape(ROWS, DE).astype(F32)
    inverse = lax.rsqrt(jnp.mean(rows * rows, axis=-1, keepdims=True) + EPS)
    inv[...] = inverse
    normed = (rows * inverse * gain_ref[...].reshape(1, DE)).astype(BF16)
    root = math.sqrt(2.0 / math.pi)
    before = dot(normed, up[...])
    square = before * before
    th = jnp.tanh(root * before * (1.0 + 0.044715 * square))
    half = 0.5 * (1.0 + th)
    slope[...] = half + 0.5 * before * (1.0 - th * th) * root * (1.0 + 3.0 * 0.044715 * square)
    return (rows + dot((before * half).astype(BF16), down[...])).astype(BF16)


def encode_back(encoded_grad, rows_ref, gain_ref, up, down, slope, inv):
    before_grad = (dot_nt(encoded_grad, down[...]) * slope[...]).astype(BF16)
    normed_grad = dot_nt(before_grad, up[...])
    rows = rows_ref[...].reshape(ROWS, DE).astype(F32)
    inverse = inv[...]
    scaled = gain_ref[...].reshape(1, DE) * normed_grad
    result = (
        encoded_grad.astype(F32)
        + inverse * scaled
        - rows
        * (inverse * inverse * inverse)
        * jnp.mean(rows * scaled, axis=-1, keepdims=True)
    )
    return result.astype(BF16)


def attention(first, count, q_all, g_all, kv, kvg, att, qg):
    zero = jnp.zeros((STRETCH, HD), BF16)
    units = [(h, i) for h in range(first, first + count) for i in range(2)]
    pairs, products, mixes = [], [], []
    for h, i in units:
        column, tokens = slice(h * HD, (h + 1) * HD), slice(i * STRETCH, (i + 1) * STRETCH)
        pair = jnp.concatenate(
            [
                jnp.concatenate([q_all[tokens, column], zero], axis=1),
                jnp.concatenate([zero, g_all[tokens, column]], axis=1),
            ],
            axis=0,
        )
        pairs.append(pair)
        products.append(dot_nt(pair, kv[h // 2, h % 2, i * NLEN : (i + 1) * NLEN, :]))
    for product in products:
        exponent = jnp.exp(product[:STRETCH] * SCALE)
        weights = exponent / jnp.sum(exponent, axis=-1, keepdims=True)
        prob_grad = product[STRETCH:]
        mean = jnp.sum(weights * prob_grad, axis=-1, keepdims=True)
        score_grad = weights * (prob_grad - mean) * SCALE
        mixes.append(jnp.concatenate([score_grad, weights], axis=0).astype(BF16))
    for (h, i), pair, mix in zip(units, pairs, mixes):
        column, tokens = slice(h * HD, (h + 1) * HD), slice(i * STRETCH, (i + 1) * STRETCH)
        keys = slice(i * NLEN, (i + 1) * NLEN)
        o = dot(mix, kv[h // 2, h % 2, keys, :])
        qg[tokens, column] = o[:STRETCH, :HD].astype(BF16)
        att[tokens, column] = o[STRETCH:, HD:].astype(BF16)
        kvg[h // 2, h % 2, keys, :] = dot_tn(mix, pair).astype(BF16)


def whole_kernel(
    slot_ref, gain_ref, pool_ref, wk_ref, wv_ref, up_ref, down_ref, q_ref, g_ref,
    att_ref, qg_ref, pg_ref, fin_ref,
    user, mid_a, mid_b, out_a, out_b, rows, wall, up, down, q_all, g_all, att, qg, slope, inv, enc, enc_other,
    enct, kv, kvg, kvg_other, part, pg,
    mid2_a, mid2_b, out2_a, out2_b, ya1, ya2, xa1, xa2, xb1, xb2, yb1, yb2,
    zbuf, fin, ssem, rsem, lsem,
):
    p = Place()
    z, c, x, y = p.z, p.c, p.x, p.y
    cp = Copies(ssem, rsem)

    def local(src, dst, index):
        return pltpu.make_async_copy(src, dst, lsem.at[index])

    def own_chunk(source):
        return local(source.at[x % 2, sub(y), :], wall.at[z, c, x, sub(y), :], 0)

    @pl.when(x < 2)
    def key_chunk():
        own_chunk(wk_ref).start()

    @pl.when(x >= 2)
    def value_chunk():
        own_chunk(wv_ref).start()

    own_slots = pl.ds(p.seq * CAP, CAP)
    mid, out = (mid_a, mid_b), (out_a, out_b)
    mid2, out2 = (mid2_a, mid2_b), (out2_a, out2_b)
    own_pool = [
        local(pool_ref.at[:, rows16(z), part_of], mid[n].at[own_slots], (1, 11)[n])
        for n, part_of in enumerate(HALVES)
    ]
    for copy in own_pool:
        copy.start()
    loads = [
        local(src, dst, 2 + n)
        for n, (src, dst) in enumerate(
            ((up_ref, up), (down_ref, down), (q_ref, q_all), (g_ref, g_all))
        )
    ]
    for load in loads:
        load.start()
    greet(
        [p.at_z(d) for d in range(1, NZ)] + [p.sibling()] + [p.at_dp(d) for d in range(1, NX * NX)]
    )

    own_chunk(wk_ref).wait()
    order = (4, 3, 5, 2, 6, 1, 7)

    def chunk(zz, xx, yy):
        return wall.at[zz, c, xx, sub(yy), :]

    pieces = ((0, 64), (64, WSUB - 64))

    def rows_of(piece):
        return pl.ds(pl.multiple_of(y * WSUB + piece[0], 16), piece[1])

    wz = [cp.start(chunk(z, x, y), chunk(z, x, y), p.at_z(d)) for d in order]
    hop1, forward = [], []
    for n, part_of in enumerate(HALVES):
        hop1.append(
            {
                d: cp.start(
                    pool_ref.at[:, rows16(p.zs(d)), part_of], mid[n].at[own_slots], p.at_z(d)
                )
                for d in order
            }
        )
        forward.append(
            [cp.start(pool_ref.at[:, rows16(z), part_of], mid[n].at[own_slots], p.sibling())]
        )

    for copy in wz:
        copy.wait_recv()
    lo, hi = pl.ds(0, 4), pl.ds(4, 4)

    def ring(region, heads, places, at):
        src = region(heads, places(0))
        return [cp.start(src, src, at(1)), cp.start(src, src, at(-1))]

    def ring2(region, first, places, at, arrived):
        arrived[0].wait_recv()
        src = region(pl.ds(first, 2), places(-1))
        one = cp.start(src, src, at(1))
        arrived[1].wait_recv()
        src = region(pl.ds(first + 2, 2), places(1))
        return [one, cp.start(src, src, at(-1))]

    def row_x(heads, xx):
        return wall.at[heads, c, xx, sub(y), :]

    def row_y(heads, yy):
        return wall.at[heads, c, x, sub(yy), :]

    def wide_y(heads, yy):
        return wall.at[heads, c, :, sub(yy), :]

    def wide_x(heads, xx):
        return wall.at[heads, c, xx, :, :]

    sib = []

    def share(src):
        sib.append(cp.start(src, src, p.sibling()))

    hop2 = []
    own_rows = [
        local(out[n].at[0], rows.at[:, rows16(z), part_of], (6, 12)[n])
        for n, part_of in enumerate(HALVES)
    ]

    def pool_step(n):
        for d in (1, 7, 2, 6, 3, 5, 4):
            hop1[n][d].wait_recv()
            block = mid[n].at[pl.ds((p.zs(-d) * 2 + c) * CAP, CAP)]
            forward[n].append(cp.start(block, block, p.sibling()))
        own_pool[n].wait()
        for copy in forward[n]:
            copy.wait_recv()
        for d in order + (0,):
            target = p.zs(d) * 2 + c
            for i in range(2):
                out[n][d, i] = mid[n][slot_ref[target * 2 + i]]
            if d == 0:
                own_rows[n].start()
            else:
                dst = rows.at[:, rows16(z), HALVES[n]]
                hop2.append(cp.start(out[n].at[d], dst, p.at_z(d)))

    a1 = ring(row_x, lo, p.xs, p.at_x)
    b1 = ring(row_y, hi, p.ys, p.at_y)
    a2 = ring2(row_x, 0, p.xs, p.at_x, a1)
    b2 = ring2(row_y, 4, p.ys, p.at_y, b1)
    for copy in a2:
        copy.wait_recv()
    a3 = ring(wide_y, lo, p.ys, p.at_y)
    for copy in b2:
        copy.wait_recv()
    b3 = ring(wide_x, hi, p.xs, p.at_x)
    share(wide_y(lo, y))
    share(wide_x(hi, x))
    def find_user(k, carry):
        slot = (p.zs(k // CAP) * 2 + c) * CAP + k % CAP
        found = jnp.int32(0)
        for stretch in range(SLOTS // 2):
            found = jnp.where(slot_ref[stretch] == slot, stretch + 1, found)
        user[k] = found
        return carry

    lax.fori_loop(0, NZ * CAP, find_user, 0)
    pool_step(0)
    a4 = ring2(wide_y, 0, p.ys, p.at_y, a3)
    b4 = ring2(wide_x, 4, p.xs, p.at_x, b3)
    for d in (1, -1):
        share(wide_y(lo, p.ys(d)))
        share(wide_x(hi, p.xs(d)))
    pool_step(1)
    for side in range(2):
        a4[side].wait_recv()
        share(wide_y(pl.ds(2 * side, 2), p.ys(2)))
        b4[side].wait_recv()
        share(wide_x(pl.ds(4 + 2 * side, 2), p.xs(2)))
    for copy in own_rows:
        copy.wait()
    for copy in hop2:
        copy.wait_recv()

    for load in loads:
        load.wait()
    encoded = encode(rows, gain_ref, up, down, slope, inv)
    enc[...] = encoded
    enc_sent = cp.start(enc, enc_other, p.sibling())
    enct[:, :ROWS] = encoded.T
    for copy in sib:
        copy.wait_recv()

    def both(h):
        k = wall[h // 2, h % 2, pl.ds(0, 2)].reshape(DE, HD)
        v = wall[h // 2, h % 2, pl.ds(2, 2)].reshape(DE, HD)
        return jnp.concatenate([k, v], axis=1)

    kvg_sent = []
    for first in range(0, HEADS, GROUP):
        for h in range(first, first + GROUP):
            kv[h // 2, h % 2] = dot(enc[...], both(h)).astype(BF16)
        attention(first, GROUP, q_all, g_all, kv, kvg, att, qg)
        span = pl.ds(first // 2, GROUP // 2)
        kvg_sent.append(cp.start(kvg.at[span, 1 - c], kvg_other.at[span], p.sibling()))
    results = [local(att, att_ref, 7), local(qg, qg_ref, 8)]
    for result in results:
        result.start()
    enc_sent.wait_recv()
    enct[:, ROWS:] = enc_other[...].T

    def weight_grad(h):
        grads = jnp.concatenate([kvg[h, c], kvg_other[h]], axis=0)
        block = dot(enct[...], grads).astype(BF16)
        for n in range(4):
            part[h, n] = block[(n % 2) * WROWS : (n % 2 + 1) * WROWS, (n // 2) * HD : (n // 2 + 1) * HD]

    def sum_y(first, count, yy):
        return part.at[pl.ds(first, count), :, sub(yy), :]

    def sum_x(first, count, xx):
        return part.at[pl.ds(first, count), xx, :, :]

    def narrow_x(first, count, xx):
        return part.at[pl.ds(first, count), xx, sub(y), :]

    def narrow_y(first, count, yy):
        return part.at[pl.ds(first, count), x, sub(yy), :]

    def far(region, first, places, at, land):
        return [
            cp.start(region(first, 2, places(2)), land.at[0], at(1)),
            cp.start(region(first + 2, 2, places(2)), land.at[1], at(-1)),
        ]

    def near(region, first, places, at, arrived, land1, land2):
        sent = []
        for side, d in ((0, 1), (1, -1)):
            arrived[side].wait_recv()
            block = region(first + 2 * side, 2, places(d))
            block[...] = (block[...].astype(F32) + land1[side].astype(F32)).astype(BF16)
            sent.append(cp.start(region(first, 4, places(d)), land2.at[side], at(d)))
        return sent

    def close(region, first, places, arrived, land2):
        for copy in arrived:
            copy.wait_recv()
        block = region(first, 4, places(0))
        block[...] = (
            block[...].astype(F32) + land2[0].astype(F32) + land2[1].astype(F32)
        ).astype(BF16)

    kvg_sent[0].wait_recv()
    for h in range(4):
        weight_grad(h)
    a1 = far(sum_y, 0, p.ys, p.at_y, ya1)
    kvg_sent[1].wait_recv()
    for h in range(4, NZ):
        weight_grad(h)
    b1 = far(sum_x, 4, p.xs, p.at_x, xb1)

    total = jnp.zeros((ROWS, DE), F32)
    for h in range(HEADS):
        total = total + dot_nt(kvg[h // 2, h % 2], both(h))
    pg[...] = encode_back(
        total.astype(BF16), rows, gain_ref, up, down, slope, inv
    ).reshape(2, NLEN, DE)

    own_two = pl.ds(p.seq * 2 + 1, 2)
    own_mid, back1, returns, back2, own_back = [], [], [], [], []

    def back_start(n):
        part_of = HALVES[n]
        own_mid.append(local(pg.at[:, rows16(z), part_of], mid2[n].at[own_two], (9, 13)[n]))
        own_mid[n].start()
        back1.append(
            {
                d: cp.start(pg.at[:, rows16(p.zs(d)), part_of], mid2[n].at[own_two], p.at_z(d))
                for d in order
            }
        )
        returns.append(
            [cp.start(pg.at[:, rows16(z), part_of], mid2[n].at[own_two], p.sibling())]
        )
        mid2[n][0] = jnp.zeros(mid2[n].shape[1:], BF16)
        own_back.append(local(out2[n].at[0], pg_ref.at[:, rows16(z), part_of], (10, 14)[n]))

    back_start(0)

    def back_step(n):
        for d in (1, 7, 2, 6, 3, 5, 4):
            back1[n][d].wait_recv()
            block = mid2[n].at[pl.ds((p.zs(-d) * 2 + c) * 2 + 1, 2)]
            returns[n].append(cp.start(block, block, p.sibling()))
        own_mid[n].wait()
        for copy in returns[n]:
            copy.wait_recv()
        for d in order + (0,):
            for j in range(CAP):
                out2[n][d, j] = mid2[n][user[d * CAP + j]]

    def back_send(n):
        for d in order + (0,):
            if d == 0:
                own_back[n].start()
            else:
                dst = pg_ref.at[:, rows16(z), HALVES[n]]
                back2.append(cp.start(out2[n].at[d], dst, p.at_z(d)))

    a2 = near(sum_y, 0, p.ys, p.at_y, a1, ya1, ya2)
    b2 = near(sum_x, 4, p.xs, p.at_x, b1, xb1, xb2)
    back_start(1)
    back_step(0)
    back_send(0)
    back_step(1)
    close(sum_y, 0, p.ys, a2, ya2)
    a3 = far(narrow_x, 0, p.xs, p.at_x, xa1)
    close(sum_x, 4, p.xs, b2, xb2)
    b3 = far(narrow_y, 4, p.ys, p.at_y, yb1)
    a4 = near(narrow_x, 0, p.xs, p.at_x, a3, xa1, xa2)
    b4 = near(narrow_y, 4, p.ys, p.at_y, b3, yb1, yb2)
    close(narrow_x, 0, p.xs, a4, xa2)
    close(narrow_y, 4, p.ys, b4, yb2)
    zsum = [
        [
            cp.start(
                part.at[p.zs(d), x, rows_of(piece), :],
                zbuf.at[d, pl.ds(*piece), :],
                p.at_z(d),
            )
            for d in order
        ]
        for piece in pieces
    ]
    back_send(1)
    last = []
    for piece, arriving in zip(pieces, zsum):
        for copy in arriving:
            copy.wait_recv()
        total = part[z, x, rows_of(piece), :].astype(F32)
        for d in range(1, NZ):
            total = total + zbuf[d, pl.ds(*piece), :].astype(F32)
        fin[x, y, pl.ds(*piece), :] = total.astype(BF16)
        block = fin.at[x, y, pl.ds(*piece), :]
        last += [cp.start(block, block, p.at_dp(d)) for d in range(1, NX * NX)]
    for copy in last:
        copy.wait_recv()
    written = local(fin, fin_ref, 15)
    written.start()
    for copy in own_back:
        copy.wait()
    for result in results:
        result.wait()
    for copy in back2:
        copy.wait_recv()
    written.wait()
    cp.finish()


def whole(slots, gain, pool, wk, wv, up, down, queries, grads):
    anyspace = pl.BlockSpec(memory_space=pl.ANY)
    vmem = pl.BlockSpec(memory_space=pltpu.VMEM)
    width = HEADS * HD

    def scratch(*shape):
        return pltpu.VMEM(shape, BF16)

    return pl.pallas_call(
        whole_kernel,
        out_shape=(
            jax.ShapeDtypeStruct((TOKENS, width), BF16),
            jax.ShapeDtypeStruct((TOKENS, width), BF16),
            jax.ShapeDtypeStruct((CAP, NLEN, DE), BF16),
            jax.ShapeDtypeStruct((NX, NX, WSUB, HD), BF16),
        ),
        in_specs=[pl.BlockSpec(memory_space=pltpu.SMEM), vmem] + [anyspace] * 7,
        out_specs=(anyspace,) * 4,
        scratch_shapes=[
            pltpu.SMEM((NZ * CAP,), jnp.int32),
            scratch(SLOTS, PIECE, SPLIT),
            scratch(SLOTS, PIECE, DE - SPLIT),
            scratch(NZ, 2, PIECE, SPLIT),
            scratch(NZ, 2, PIECE, DE - SPLIT),
            scratch(2, NLEN, DE),
            scratch(NZ, 2, 4, WROWS, HD),
            scratch(DE, FFE),
            scratch(FFE, DE),
            scratch(TOKENS, width),
            scratch(TOKENS, width),
            scratch(TOKENS, width),
            scratch(TOKENS, width),
            pltpu.VMEM((ROWS, FFE), F32),
            pltpu.VMEM((ROWS, 1), F32),
            scratch(ROWS, DE),
            scratch(ROWS, DE),
            scratch(DE, 2 * ROWS),
            scratch(NZ, 2, ROWS, 2 * HD),
            scratch(NZ, 2, ROWS, 2 * HD),
            scratch(NZ, ROWS, 2 * HD),
            scratch(NZ, 4, WROWS, HD),
            scratch(2, NLEN, DE),
            scratch(1 + SLOTS // 2, PIECE, SPLIT),
            scratch(1 + SLOTS // 2, PIECE, DE - SPLIT),
            scratch(NZ, CAP, PIECE, SPLIT),
            scratch(NZ, CAP, PIECE, DE - SPLIT),
            scratch(2, 2, 4, WSUB, HD),
            scratch(2, 4, 4, WSUB, HD),
            scratch(2, 2, WSUB, HD),
            scratch(2, 4, WSUB, HD),
            scratch(2, 2, WROWS, HD),
            scratch(2, 4, WROWS, HD),
            scratch(2, 2, WSUB, HD),
            scratch(2, 4, WSUB, HD),
            scratch(NZ, WSUB, HD),
            scratch(NX, NX, WSUB, HD),
            pltpu.SemaphoreType.DMA((COPIES,)),
            pltpu.SemaphoreType.DMA((COPIES,)),
            pltpu.SemaphoreType.DMA((16,)),
        ],
        compiler_params=pltpu.CompilerParams(
            collective_id=0, has_side_effects=True, vmem_limit_bytes=56 * 1024 * 1024
        ),
        name="whole",
    )(slots, gain, pool, wk, wv, up, down, queries, grads)


def place_kernel(
    att, qg, pg, fin, att_out, qg_out, pg_out, kw_out, vw_out,
    wide, key, value, att_held, qg_held, pg_held, sems,
):
    loads, stores = [], []

    def move(src, held, dst):
        loads.append(pltpu.make_async_copy(src, held, sems.at[len(loads)]))
        stores.append(pltpu.make_async_copy(held, dst, sems.at[16 + len(stores)]))
        loads[-1].start()

    wide_load = pltpu.make_async_copy(fin, wide, sems.at[15])
    wide_load.start()
    for src, held, dst, cut in (
        (pg, pg_held, pg_out, 4),
        (att, att_held, att_out, 2),
        (qg, qg_held, qg_out, 2),
    ):
        size = src.shape[0] // cut
        for n in range(cut):
            span = pl.ds(n * size, size)
            move(src.at[span], held.at[span], dst.at[span])
    wide_load.wait()
    for n, (held, dst) in enumerate(((key, kw_out), (value, vw_out))):
        held[...] = wide[2 * n : 2 * n + 2].reshape(DE, HD).astype(F32)
        stores.append(pltpu.make_async_copy(held, dst, sems.at[16 + len(stores)]))
        stores[-1].start()
    for load, store in zip(loads, stores):
        load.wait()
        store.start()
    for store in stores:
        store.wait()


def place(att, qg, pg, fin):
    anyspace = pl.BlockSpec(memory_space=pl.ANY)
    shapes = [jax.ShapeDtypeStruct(a.shape, a.dtype) for a in (att, qg, pg)]
    grad = jax.ShapeDtypeStruct((DE, HD), F32)
    return pl.pallas_call(
        place_kernel,
        out_shape=(*shapes, grad, grad),
        in_specs=[anyspace] * 4,
        out_specs=(anyspace,) * 5,
        scratch_shapes=[
            pltpu.VMEM((NX, NX, WSUB, HD), BF16),
            pltpu.VMEM((DE, HD), F32),
            pltpu.VMEM((DE, HD), F32),
            pltpu.VMEM(att.shape, BF16),
            pltpu.VMEM(qg.shape, BF16),
            pltpu.VMEM(pg.shape, BF16),
            pltpu.SemaphoreType.DMA((32,)),
        ],
        compiler_params=pltpu.CompilerParams(vmem_limit_bytes=56 * 1024 * 1024),
        name="place",
    )(att, qg, pg, fin)


def on_device(queries, attended_grad, pool, stretch_slot, gain, up, down, key_w, value_w):
    attended, query_grad, pool_grad, key_grad, value_grad = place(
        *whole(
            stretch_slot[0],
            gain,
            pool[0],
            key_w.reshape(2, WROWS, HD),
            value_w.reshape(2, WROWS, HD),
            up,
            down,
            queries[0],
            attended_grad[0],
        )
    )
    return attended[None], query_grad[None], pool_grad[None], key_grad, value_grad


def solution(mesh):
    return jax.shard_map(
        on_device,
        mesh=mesh,
        in_specs=(
            P("dp", "seq", None),
            P("dp", "seq", None),
            P("dp", "seq", None, None),
            P("dp", None),
            P(),
            P(),
            P(),
            P(None, "seq"),
            P(None, "seq"),
        ),
        out_specs=(
            P("dp", "seq", None),
            P("dp", "seq", None),
            P("dp", "seq", None, None),
            P(None, "seq"),
            P(None, "seq"),
        ),
        check_vma=False,
    )
```

```python
import math

import jax
import jax.numpy as jnp
from jax import lax
from jax.experimental import pallas as pl
from jax.experimental.pallas import tpu as pltpu
from jax.sharding import PartitionSpec as P

STRETCH = 64
HD = 128
NX = 4
NZ = 8
CAP = 4
SLOTS = 64
NLEN = 128
PIECE = 16
DE = 896
FFE = 1792
HEADS = 16
WROWS = 448
WSUB = 112
TOKENS = 128
EPS = 1e-6
SCALE = 1.0 / math.sqrt(HD)

MESH = pl.DeviceIdType.MESH
BF16 = jnp.bfloat16
F32 = jnp.float32


class Place:
    def __init__(self):
        self.dp = lax.axis_index("dp")
        self.seq = lax.axis_index("seq")
        self.x = self.dp // NX
        self.y = self.dp % NX
        self.z = self.seq // 2
        self.c = self.seq % 2

    def xs(self, d):
        return (self.x + d + NX) % NX

    def ys(self, d):
        return (self.y + d + NX) % NX

    def zs(self, d):
        return (self.z + d + NZ) % NZ

    def at_x(self, d):
        return (self.xs(d) * NX + self.y, self.seq)

    def at_y(self, d):
        return (self.x * NX + self.ys(d), self.seq)

    def at_z(self, d):
        return (self.dp, self.zs(d) * 2 + self.c)

    def at_dp(self, d):
        return ((self.dp + d) % (NX * NX), self.seq)

    def sibling(self):
        return (self.dp, self.z * 2 + 1 - self.c)


def greet(partners):
    barrier = pltpu.get_barrier_semaphore()
    for partner in partners:
        pl.semaphore_signal(barrier, inc=1, device_id=partner, device_id_type=MESH)
    pl.semaphore_wait(barrier, len(partners))


class Copies:
    def __init__(self, send_sems, recv_sems):
        self.send_sems, self.recv_sems = send_sems, recv_sems
        self.count = 0
        self.all = []

    def start(self, src, dst, device):
        copy = pltpu.make_async_remote_copy(
            src_ref=src,
            dst_ref=dst,
            send_sem=self.send_sems.at[self.count],
            recv_sem=self.recv_sems.at[self.count],
            device_id=device,
            device_id_type=MESH,
        )
        self.count += 1
        self.all.append(copy)
        copy.start()
        return copy

    def finish(self):
        for copy in self.all:
            copy.wait_send()


def rows16(index):
    return pl.ds(pl.multiple_of(index * PIECE, PIECE), PIECE)


def sub(index):
    return pl.ds(pl.multiple_of(index * WSUB, 16), WSUB)


COPIES = 192
SPLIT = 512
HALVES = (slice(0, SPLIT), slice(SPLIT, DE))
GROUP = 8
TILE = 256
ROWS = 2 * NLEN


def dot(a, b):
    return jnp.dot(a, b, preferred_element_type=F32)


def dot_nt(a, b):
    return lax.dot_general(a, b, (((1,), (1,)), ((), ())), preferred_element_type=F32)


def dot_tn(a, b):
    return lax.dot_general(a, b, (((0,), (0,)), ((), ())), preferred_element_type=F32)


def encode(rows_ref, gain_ref, up, down, slope, inv):
    rows = rows_ref[...].reshape(ROWS, DE).astype(F32)
    inverse = lax.rsqrt(jnp.mean(rows * rows, axis=-1, keepdims=True) + EPS)
    inv[...] = inverse
    normed = (rows * inverse * gain_ref[...].reshape(1, DE)).astype(BF16)
    root = math.sqrt(2.0 / math.pi)
    before = dot(normed, up[...])
    square = before * before
    th = jnp.tanh(root * before * (1.0 + 0.044715 * square))
    half = 0.5 * (1.0 + th)
    slope[...] = half + 0.5 * before * (1.0 - th * th) * root * (1.0 + 3.0 * 0.044715 * square)
    return (rows + dot((before * half).astype(BF16), down[...])).astype(BF16)


def encode_back(encoded_grad, rows_ref, gain_ref, up, down, slope, inv):
    before_grad = (dot_nt(encoded_grad, down[...]) * slope[...]).astype(BF16)
    normed_grad = dot_nt(before_grad, up[...])
    rows = rows_ref[...].reshape(ROWS, DE).astype(F32)
    inverse = inv[...]
    scaled = gain_ref[...].reshape(1, DE) * normed_grad
    result = (
        encoded_grad.astype(F32)
        + inverse * scaled
        - rows
        * (inverse * inverse * inverse)
        * jnp.mean(rows * scaled, axis=-1, keepdims=True)
    )
    return result.astype(BF16)


def attention(first, count, q_all, g_all, kv, kvg, att, qg):
    zero = jnp.zeros((STRETCH, HD), BF16)
    units = [(h, i) for h in range(first, first + count) for i in range(2)]
    pairs, products, mixes = [], [], []
    for h, i in units:
        column, tokens = slice(h * HD, (h + 1) * HD), slice(i * STRETCH, (i + 1) * STRETCH)
        pair = jnp.concatenate(
            [
                jnp.concatenate([q_all[tokens, column], zero], axis=1),
                jnp.concatenate([zero, g_all[tokens, column]], axis=1),
            ],
            axis=0,
        )
        pairs.append(pair)
        products.append(dot_nt(pair, kv[h // 2, h % 2, i * NLEN : (i + 1) * NLEN, :]))
    for product in products:
        exponent = jnp.exp(product[:STRETCH] * SCALE)
        weights = exponent / jnp.sum(exponent, axis=-1, keepdims=True)
        prob_grad = product[STRETCH:]
        mean = jnp.sum(weights * prob_grad, axis=-1, keepdims=True)
        score_grad = weights * (prob_grad - mean) * SCALE
        mixes.append(jnp.concatenate([score_grad, weights], axis=0).astype(BF16))
    for (h, i), pair, mix in zip(units, pairs, mixes):
        column, tokens = slice(h * HD, (h + 1) * HD), slice(i * STRETCH, (i + 1) * STRETCH)
        keys = slice(i * NLEN, (i + 1) * NLEN)
        o = dot(mix, kv[h // 2, h % 2, keys, :])
        qg[tokens, column] = o[:STRETCH, :HD].astype(BF16)
        att[tokens, column] = o[STRETCH:, HD:].astype(BF16)
        kvg[h // 2, h % 2, keys, :] = dot_tn(mix, pair).astype(BF16)


def whole_kernel(
    slot_ref, gain_ref, pool_ref, wk_ref, wv_ref, up_ref, down_ref, q_ref, g_ref,
    att_ref, qg_ref, pg_ref, fin_ref,
    user, mid_a, mid_b, out_a, out_b, rows, wall, up, down, q_all, g_all, att, qg, slope, inv, enc, enc_other,
    enct, kv, kvg, kvg_other, part, pg,
    mid2_a, mid2_b, out2_a, out2_b, ya1, ya2, xa1, xa2, xb1, xb2, yb1, yb2,
    zbuf, fin, ssem, rsem, lsem,
):
    p = Place()
    z, c, x, y = p.z, p.c, p.x, p.y
    cp = Copies(ssem, rsem)

    def local(src, dst, index):
        return pltpu.make_async_copy(src, dst, lsem.at[index])

    def own_chunk(source):
        return local(source.at[x % 2, sub(y), :], wall.at[z, c, x, sub(y), :], 0)

    @pl.when(x < 2)
    def key_chunk():
        own_chunk(wk_ref).start()

    @pl.when(x >= 2)
    def value_chunk():
        own_chunk(wv_ref).start()

    own_slots = pl.ds(p.seq * CAP, CAP)
    mid, out = (mid_a, mid_b), (out_a, out_b)
    mid2, out2 = (mid2_a, mid2_b), (out2_a, out2_b)
    own_pool = [
        local(pool_ref.at[:, rows16(z), part_of], mid[n].at[own_slots], (1, 11)[n])
        for n, part_of in enumerate(HALVES)
    ]
    for copy in own_pool:
        copy.start()
    loads = [
        local(src, dst, 2 + n)
        for n, (src, dst) in enumerate(
            ((up_ref, up), (down_ref, down), (q_ref, q_all), (g_ref, g_all))
        )
    ]
    for load in loads:
        load.start()
    greet(
        [p.at_z(d) for d in range(1, NZ)] + [p.sibling()] + [p.at_dp(d) for d in range(1, NX * NX)]
    )

    own_chunk(wk_ref).wait()
    order = (4, 3, 5, 2, 6, 1, 7)

    def chunk(zz, xx, yy):
        return wall.at[zz, c, xx, sub(yy), :]

    pieces = ((0, 64), (64, WSUB - 64))

    def rows_of(piece):
        return pl.ds(pl.multiple_of(y * WSUB + piece[0], 16), piece[1])

    wz = [cp.start(chunk(z, x, y), chunk(z, x, y), p.at_z(d)) for d in order]
    hop1, forward = [], []
    for n, part_of in enumerate(HALVES):
        hop1.append(
            {
                d: cp.start(
                    pool_ref.at[:, rows16(p.zs(d)), part_of], mid[n].at[own_slots], p.at_z(d)
                )
                for d in order
            }
        )
        forward.append(
            [cp.start(pool_ref.at[:, rows16(z), part_of], mid[n].at[own_slots], p.sibling())]
        )

    for copy in wz:
        copy.wait_recv()
    lo, hi = pl.ds(0, 4), pl.ds(4, 4)

    def ring(region, heads, places, at):
        src = region(heads, places(0))
        return [cp.start(src, src, at(1)), cp.start(src, src, at(-1))]

    def ring2(region, first, places, at, arrived):
        arrived[0].wait_recv()
        src = region(pl.ds(first, 2), places(-1))
        one = cp.start(src, src, at(1))
        arrived[1].wait_recv()
        src = region(pl.ds(first + 2, 2), places(1))
        return [one, cp.start(src, src, at(-1))]

    def row_x(heads, xx):
        return wall.at[heads, c, xx, sub(y), :]

    def row_y(heads, yy):
        return wall.at[heads, c, x, sub(yy), :]

    def wide_y(heads, yy):
        return wall.at[heads, c, :, sub(yy), :]

    def wide_x(heads, xx):
        return wall.at[heads, c, xx, :, :]

    sib = []

    def share(src):
        sib.append(cp.start(src, src, p.sibling()))

    hop2 = []
    own_rows = [
        local(out[n].at[0], rows.at[:, rows16(z), part_of], (6, 12)[n])
        for n, part_of in enumerate(HALVES)
    ]

    def pool_step(n):
        for d in (1, 7, 2, 6, 3, 5, 4):
            hop1[n][d].wait_recv()
            block = mid[n].at[pl.ds((p.zs(-d) * 2 + c) * CAP, CAP)]
            forward[n].append(cp.start(block, block, p.sibling()))
        own_pool[n].wait()
        for copy in forward[n]:
            copy.wait_recv()
        for d in order + (0,):
            target = p.zs(d) * 2 + c
            for i in range(2):
                out[n][d, i] = mid[n][slot_ref[target * 2 + i]]
            if d == 0:
                own_rows[n].start()
            else:
                dst = rows.at[:, rows16(z), HALVES[n]]
                hop2.append(cp.start(out[n].at[d], dst, p.at_z(d)))

    a1 = ring(row_x, lo, p.xs, p.at_x)
    b1 = ring(row_y, hi, p.ys, p.at_y)
    a2 = ring2(row_x, 0, p.xs, p.at_x, a1)
    b2 = ring2(row_y, 4, p.ys, p.at_y, b1)
    for copy in a2:
        copy.wait_recv()
    a3 = ring(wide_y, lo, p.ys, p.at_y)
    for copy in b2:
        copy.wait_recv()
    b3 = ring(wide_x, hi, p.xs, p.at_x)
    share(wide_y(lo, y))
    share(wide_x(hi, x))
    def find_user(k, carry):
        slot = (p.zs(k // CAP) * 2 + c) * CAP + k % CAP
        found = jnp.int32(0)
        for stretch in range(SLOTS // 2):
            found = jnp.where(slot_ref[stretch] == slot, stretch + 1, found)
        user[k] = found
        return carry

    lax.fori_loop(0, NZ * CAP, find_user, 0)
    pool_step(0)
    a4 = ring2(wide_y, 0, p.ys, p.at_y, a3)
    b4 = ring2(wide_x, 4, p.xs, p.at_x, b3)
    for d in (1, -1):
        share(wide_y(lo, p.ys(d)))
        share(wide_x(hi, p.xs(d)))
    pool_step(1)
    for side in range(2):
        a4[side].wait_recv()
        share(wide_y(pl.ds(2 * side, 2), p.ys(2)))
        b4[side].wait_recv()
        share(wide_x(pl.ds(4 + 2 * side, 2), p.xs(2)))
    for copy in own_rows:
        copy.wait()
    for copy in hop2:
        copy.wait_recv()

    for load in loads:
        load.wait()
    encoded = encode(rows, gain_ref, up, down, slope, inv)
    enc[...] = encoded
    enc_sent = cp.start(enc, enc_other, p.sibling())
    enct[:, :ROWS] = encoded.T
    for copy in sib:
        copy.wait_recv()

    def both(h):
        k = wall[h // 2, h % 2, pl.ds(0, 2)].reshape(DE, HD)
        v = wall[h // 2, h % 2, pl.ds(2, 2)].reshape(DE, HD)
        return jnp.concatenate([k, v], axis=1)

    kvg_sent = []
    for first in range(0, HEADS, GROUP):
        for h in range(first, first + GROUP):
            kv[h // 2, h % 2] = dot(enc[...], both(h)).astype(BF16)
        attention(first, GROUP, q_all, g_all, kv, kvg, att, qg)
        span = pl.ds(first // 2, GROUP // 2)
        kvg_sent.append(cp.start(kvg.at[span, 1 - c], kvg_other.at[span], p.sibling()))
    results = [local(att, att_ref, 7), local(qg, qg_ref, 8)]
    for result in results:
        result.start()
    enc_sent.wait_recv()
    enct[:, ROWS:] = enc_other[...].T

    def weight_grad(h):
        grads = jnp.concatenate([kvg[h, c], kvg_other[h]], axis=0)
        block = dot(enct[...], grads).astype(BF16)
        for n in range(4):
            part[h, n] = block[(n % 2) * WROWS : (n % 2 + 1) * WROWS, (n // 2) * HD : (n // 2 + 1) * HD]

    def sum_y(first, count, yy):
        return part.at[pl.ds(first, count), :, sub(yy), :]

    def sum_x(first, count, xx):
        return part.at[pl.ds(first, count), xx, :, :]

    def narrow_x(first, count, xx):
        return part.at[pl.ds(first, count), xx, sub(y), :]

    def narrow_y(first, count, yy):
        return part.at[pl.ds(first, count), x, sub(yy), :]

    def far(region, first, places, at, land):
        return [
            cp.start(region(first, 2, places(2)), land.at[0], at(1)),
            cp.start(region(first + 2, 2, places(2)), land.at[1], at(-1)),
        ]

    def near(region, first, places, at, arrived, land1, land2):
        sent = []
        for side, d in ((0, 1), (1, -1)):
            arrived[side].wait_recv()
            block = region(first + 2 * side, 2, places(d))
            block[...] = (block[...].astype(F32) + land1[side].astype(F32)).astype(BF16)
            sent.append(cp.start(region(first, 4, places(d)), land2.at[side], at(d)))
        return sent

    def close(region, first, places, arrived, land2):
        for copy in arrived:
            copy.wait_recv()
        block = region(first, 4, places(0))
        block[...] = (
            block[...].astype(F32) + land2[0].astype(F32) + land2[1].astype(F32)
        ).astype(BF16)

    kvg_sent[0].wait_recv()
    for h in range(4):
        weight_grad(h)
    a1 = far(sum_y, 0, p.ys, p.at_y, ya1)
    kvg_sent[1].wait_recv()
    for h in range(4, NZ):
        weight_grad(h)
    b1 = far(sum_x, 4, p.xs, p.at_x, xb1)

    total = jnp.zeros((ROWS, DE), F32)
    for h in range(HEADS):
        total = total + dot_nt(kvg[h // 2, h % 2], both(h))
    pg[...] = encode_back(
        total.astype(BF16), rows, gain_ref, up, down, slope, inv
    ).reshape(2, NLEN, DE)

    own_two = pl.ds(p.seq * 2 + 1, 2)
    own_mid, back1, returns, back2, own_back = [], [], [], [], []

    def back_start(n):
        part_of = HALVES[n]
        own_mid.append(local(pg.at[:, rows16(z), part_of], mid2[n].at[own_two], (9, 13)[n]))
        own_mid[n].start()
        back1.append(
            {
                d: cp.start(pg.at[:, rows16(p.zs(d)), part_of], mid2[n].at[own_two], p.at_z(d))
                for d in order
            }
        )
        returns.append(
            [cp.start(pg.at[:, rows16(z), part_of], mid2[n].at[own_two], p.sibling())]
        )
        mid2[n][0] = jnp.zeros(mid2[n].shape[1:], BF16)
        own_back.append(local(out2[n].at[0], pg_ref.at[:, rows16(z), part_of], (10, 14)[n]))

    back_start(0)

    def back_step(n):
        for d in (1, 7, 2, 6, 3, 5, 4):
            back1[n][d].wait_recv()
            block = mid2[n].at[pl.ds((p.zs(-d) * 2 + c) * 2 + 1, 2)]
            returns[n].append(cp.start(block, block, p.sibling()))
        own_mid[n].wait()
        for copy in returns[n]:
            copy.wait_recv()
        for d in order + (0,):
            for j in range(CAP):
                out2[n][d, j] = mid2[n][user[d * CAP + j]]

    def back_send(n):
        for d in order + (0,):
            if d == 0:
                own_back[n].start()
            else:
                dst = pg_ref.at[:, rows16(z), HALVES[n]]
                back2.append(cp.start(out2[n].at[d], dst, p.at_z(d)))

    a2 = near(sum_y, 0, p.ys, p.at_y, a1, ya1, ya2)
    b2 = near(sum_x, 4, p.xs, p.at_x, b1, xb1, xb2)
    back_start(1)
    back_step(0)
    back_send(0)
    back_step(1)
    close(sum_y, 0, p.ys, a2, ya2)
    a3 = far(narrow_x, 0, p.xs, p.at_x, xa1)
    close(sum_x, 4, p.xs, b2, xb2)
    b3 = far(narrow_y, 4, p.ys, p.at_y, yb1)
    a4 = near(narrow_x, 0, p.xs, p.at_x, a3, xa1, xa2)
    b4 = near(narrow_y, 4, p.ys, p.at_y, b3, yb1, yb2)
    close(narrow_x, 0, p.xs, a4, xa2)
    close(narrow_y, 4, p.ys, b4, yb2)
    zsum = [
        [
            cp.start(
                part.at[p.zs(d), x, rows_of(piece), :],
                zbuf.at[d, pl.ds(*piece), :],
                p.at_z(d),
            )
            for d in order
        ]
        for piece in pieces
    ]
    back_send(1)
    last = []
    for piece, arriving in zip(pieces, zsum):
        for copy in arriving:
            copy.wait_recv()
        total = part[z, x, rows_of(piece), :].astype(F32)
        for d in range(1, NZ):
            total = total + zbuf[d, pl.ds(*piece), :].astype(F32)
        fin[x, y, pl.ds(*piece), :] = total.astype(BF16)
        block = fin.at[x, y, pl.ds(*piece), :]
        last += [cp.start(block, block, p.at_dp(d)) for d in range(1, NX * NX)]
    for copy in last:
        copy.wait_recv()
    written = local(fin, fin_ref, 15)
    written.start()
    for copy in own_back:
        copy.wait()
    for result in results:
        result.wait()
    for copy in back2:
        copy.wait_recv()
    written.wait()
    cp.finish()


def whole(slots, gain, pool, wk, wv, up, down, queries, grads):
    anyspace = pl.BlockSpec(memory_space=pl.ANY)
    vmem = pl.BlockSpec(memory_space=pltpu.VMEM)
    width = HEADS * HD

    def scratch(*shape):
        return pltpu.VMEM(shape, BF16)

    return pl.pallas_call(
        whole_kernel,
        out_shape=(
            jax.ShapeDtypeStruct((TOKENS, width), BF16),
            jax.ShapeDtypeStruct((TOKENS, width), BF16),
            jax.ShapeDtypeStruct((CAP, NLEN, DE), BF16),
            jax.ShapeDtypeStruct((NX, NX, WSUB, HD), BF16),
        ),
        in_specs=[pl.BlockSpec(memory_space=pltpu.SMEM), vmem] + [anyspace] * 7,
        out_specs=(anyspace,) * 4,
        scratch_shapes=[
            pltpu.SMEM((NZ * CAP,), jnp.int32),
            scratch(SLOTS, PIECE, SPLIT),
            scratch(SLOTS, PIECE, DE - SPLIT),
            scratch(NZ, 2, PIECE, SPLIT),
            scratch(NZ, 2, PIECE, DE - SPLIT),
            scratch(2, NLEN, DE),
            scratch(NZ, 2, 4, WROWS, HD),
            scratch(DE, FFE),
            scratch(FFE, DE),
            scratch(TOKENS, width),
            scratch(TOKENS, width),
            scratch(TOKENS, width),
            scratch(TOKENS, width),
            pltpu.VMEM((ROWS, FFE), F32),
            pltpu.VMEM((ROWS, 1), F32),
            scratch(ROWS, DE),
            scratch(ROWS, DE),
            scratch(DE, 2 * ROWS),
            scratch(NZ, 2, ROWS, 2 * HD),
            scratch(NZ, 2, ROWS, 2 * HD),
            scratch(NZ, ROWS, 2 * HD),
            scratch(NZ, 4, WROWS, HD),
            scratch(2, NLEN, DE),
            scratch(1 + SLOTS // 2, PIECE, SPLIT),
            scratch(1 + SLOTS // 2, PIECE, DE - SPLIT),
            scratch(NZ, CAP, PIECE, SPLIT),
            scratch(NZ, CAP, PIECE, DE - SPLIT),
            scratch(2, 2, 4, WSUB, HD),
            scratch(2, 4, 4, WSUB, HD),
            scratch(2, 2, WSUB, HD),
            scratch(2, 4, WSUB, HD),
            scratch(2, 2, WROWS, HD),
            scratch(2, 4, WROWS, HD),
            scratch(2, 2, WSUB, HD),
            scratch(2, 4, WSUB, HD),
            scratch(NZ, WSUB, HD),
            scratch(NX, NX, WSUB, HD),
            pltpu.SemaphoreType.DMA((COPIES,)),
            pltpu.SemaphoreType.DMA((COPIES,)),
            pltpu.SemaphoreType.DMA((16,)),
        ],
        compiler_params=pltpu.CompilerParams(
            collective_id=0, has_side_effects=True, vmem_limit_bytes=56 * 1024 * 1024
        ),
        name="whole",
    )(slots, gain, pool, wk, wv, up, down, queries, grads)


def place_kernel(
    att, qg, pg, fin, att_out, qg_out, pg_out, kw_out, vw_out,
    wide, key, value, att_held, qg_held, pg_held, sems,
):
    loads, stores = [], []

    def move(src, held, dst):
        loads.append(pltpu.make_async_copy(src, held, sems.at[len(loads)]))
        stores.append(pltpu.make_async_copy(held, dst, sems.at[16 + len(stores)]))
        loads[-1].start()

    wide_load = pltpu.make_async_copy(fin, wide, sems.at[15])
    wide_load.start()
    for src, held, dst, cut in (
        (pg, pg_held, pg_out, 4),
        (att, att_held, att_out, 2),
        (qg, qg_held, qg_out, 2),
    ):
        size = src.shape[0] // cut
        for n in range(cut):
            span = pl.ds(n * size, size)
            move(src.at[span], held.at[span], dst.at[span])
    wide_load.wait()
    for n, (held, dst) in enumerate(((key, kw_out), (value, vw_out))):
        held[...] = wide[2 * n : 2 * n + 2].reshape(DE, HD).astype(F32)
        stores.append(pltpu.make_async_copy(held, dst, sems.at[16 + len(stores)]))
        stores[-1].start()
    for load, store in zip(loads, stores):
        load.wait()
        store.start()
    for store in stores:
        store.wait()


def place(att, qg, pg, fin):
    anyspace = pl.BlockSpec(memory_space=pl.ANY)
    shapes = [jax.ShapeDtypeStruct(a.shape, a.dtype) for a in (att, qg, pg)]
    grad = jax.ShapeDtypeStruct((DE, HD), F32)
    return pl.pallas_call(
        place_kernel,
        out_shape=(*shapes, grad, grad),
        in_specs=[anyspace] * 4,
        out_specs=(anyspace,) * 5,
        scratch_shapes=[
            pltpu.VMEM((NX, NX, WSUB, HD), BF16),
            pltpu.VMEM((DE, HD), F32),
            pltpu.VMEM((DE, HD), F32),
            pltpu.VMEM(att.shape, BF16),
            pltpu.VMEM(qg.shape, BF16),
            pltpu.VMEM(pg.shape, BF16),
            pltpu.SemaphoreType.DMA((32,)),
        ],
        compiler_params=pltpu.CompilerParams(vmem_limit_bytes=56 * 1024 * 1024),
        name="place",
    )(att, qg, pg, fin)


def on_device(queries, attended_grad, pool, stretch_slot, gain, up, down, key_w, value_w):
    attended, query_grad, pool_grad, key_grad, value_grad = place(
        *whole(
            stretch_slot[0],
            gain,
            pool[0],
            key_w.reshape(2, WROWS, HD),
            value_w.reshape(2, WROWS, HD),
            up,
            down,
            queries[0],
            attended_grad[0],
        )
    )
    return attended[None], query_grad[None], pool_grad[None], key_grad, value_grad


def solution(mesh):
    return jax.shard_map(
        on_device,
        mesh=mesh,
        in_specs=(
            P("dp", "seq", None),
            P("dp", "seq", None),
            P("dp", "seq", None, None),
            P("dp", None),
            P(),
            P(),
            P(),
            P(None, "seq"),
            P(None, "seq"),
        ),
        out_specs=(
            P("dp", "seq", None),
            P("dp", "seq", None),
            P("dp", "seq", None, None),
            P(None, "seq"),
            P(None, "seq"),
        ),
        check_vma=False,
    )
```
